128 devices in a mesh: section: 8 (over x_lo, z), tensor: 16 (over y, x_hi, core).
Axes of the slice: x: 4 (x_hi: 2, x_lo: 2; x = x_hi * 2 + x_lo), y: 4, z: 4, core: 2. Of those that a mesh axis runs over, the one named last changes fastest.
Arguments:
- hidden_in: bfloat16 [8, 1024, 8192], P('section', 'tensor'), may hold values from -6 to 6
- norm_gain: bfloat16 [8, 8192], P('section'), may hold values from 0.5 to 1.5
- w_query: bfloat16 [8, 8192, 8192], P('section', None, 'tensor')
- bias_query: bfloat16 [8, 8192], P('section', 'tensor'), may hold values from -3 to 3
- w_key: bfloat16 [8, 8192, 1024], P('section', 'tensor')
- w_value: bfloat16 [8, 8192, 1024], P('section', 'tensor'), may hold values from -0.0625 to 0.0625
- bias_value: bfloat16 [8, 1024], P('section'), may hold values from -3 to 3
- w_out: bfloat16 [8, 8192, 8192], P('section', 'tensor'), may hold values from -0.0625 to 0.0625
- visible_end: int32 [8, 1024], P('section'), may hold values from 1 to 1024, as said below
Outputs:
- handed: bfloat16 [8, 1024, 8192], P('section', 'tensor')
The draws below stay inside these ranges and needn't reach their ends.
Inputs may be any that keep to these rules, and one draw needn't show every extreme that they name: Token i attends keys j < visible_end[s, i]; visible_end[s, i] >= i + 1; the tokens of one frame segment share the end of their segment, an instruction token i has i + 1, and the last token has 1024.
All inputs are finite; a program needn't handle non-finite values.
Results may differ from the reference program's by a relative error of at most 0.015.
Values may be sent and summed in bfloat16 or wider, within the bound.
A program may use at most 128 MiB of HBM per device.

```python
import jax
import jax.numpy as jnp
from jax import lax

D = 8192
HEADS = 64
KV = 8
HEAD = 128
TOKENS = 1024
SECTIONS = 8
N_TENSOR = 16


def key_columns(key):
    return jax.random.normal(key, (SECTIONS, D, KV * HEAD), jnp.float32) * D ** (-0.5)


def draw_w_key(key, part):
    return key_columns(key).astype(jnp.bfloat16)


def draw_w_query(key, part):
    key = jax.random.fold_in(key, 7)
    noise_key = jax.random.fold_in(key, 0)
    noise = jax.random.normal(noise_key, (SECTIONS, D, HEADS * HEAD), jnp.float32) * D ** (-0.5)
    return noise.astype(jnp.bfloat16)


def draw_visible_end(key, part):
    key = jax.random.fold_in(key, 3)
    bound_key, kind_key = jax.random.split(key)
    place = jnp.arange(TOKENS, dtype=jnp.int32)[None, :]
    boundary = (jax.random.randint(bound_key, (SECTIONS, TOKENS), 0, 96) == 0) | (place == TOKENS - 1)
    flags = boundary.astype(jnp.int32)
    segment = jnp.cumsum(flags, axis=1) - flags
    kinds = jax.random.randint(kind_key, (SECTIONS, TOKENS), 0, 2)
    frame = (jnp.take_along_axis(kinds, segment, axis=1) == 1) & (segment > 0)
    closing = jnp.where(boundary, place + 1, TOKENS)
    segment_end = lax.cummin(closing, axis=1, reverse=True)
    return jnp.where(frame, segment_end, place + 1).astype(jnp.int32)


def block_levels(rng, dims, cuts, smallest, largest):
    loudness, own = 1.0, jax.random.fold_in(rng, 6)
    for axis_at, shards_of in cuts:
        draws = jnp.exp(jax.random.uniform(jax.random.fold_in(own, axis_at), (shards_of,), jnp.float32, smallest / len(cuts), largest / len(cuts)))
        loudness = loudness * jnp.repeat(draws, dims[axis_at] // shards_of).reshape([-1 if axis == axis_at else 1 for axis in range(len(dims))])
    return loudness


def centred(key, dims, scale, limit, cuts=(), kind=jnp.bfloat16):
    array = scale * jax.random.normal(key, dims, jnp.float32)
    if cuts:
        array = array * block_levels(key, dims, cuts, -0.22, 0.18)
    return jnp.clip(array, -limit, limit).astype(kind)


def setup_inputs(seed: int = 0) -> dict:
    key_of = jax.random.split(jax.random.key(seed), 10)
    hidden_in = centred(key_of[0], (SECTIONS, TOKENS, D), 1.0, 6.0, ((0, 8), (1, 16)))
    norm_gain = jnp.clip(1.0 + 0.1 * jax.random.normal(key_of[1], (SECTIONS, D), jnp.float32), 0.5, 1.5).astype(jnp.bfloat16)
    w_query = draw_w_query(jax.random.fold_in(key_of[9], 71), 0)
    bias_query = centred(key_of[3], (SECTIONS, HEADS * HEAD), 0.5, 3.0, ((0, 8), (1, 16)))
    w_key = draw_w_key(jax.random.fold_in(key_of[9], 71), 0)
    w_value = centred(key_of[5], (SECTIONS, D, KV * HEAD), D ** -0.5, 0.0625, ((0, 8), (1, 16)))
    bias_value = centred(key_of[6], (SECTIONS, KV * HEAD), 0.5, 3.0, ((0, 8),))
    w_out = centred(key_of[7], (SECTIONS, HEADS * HEAD, D), (HEADS * HEAD) ** -0.5, 0.0625, ((0, 8), (1, 16)))
    visible_end = draw_visible_end(jax.random.fold_in(key_of[9], 71), 0)
    return {"hidden_in": hidden_in, "norm_gain": norm_gain, "w_query": w_query, "bias_query": bias_query, "w_key": w_key, "w_value": w_value, "bias_value": bias_value, "w_out": w_out, "visible_end": visible_end}


def normalize(rows, gain):
    values = rows.astype(jnp.float32)
    power = lax.optimization_barrier(jnp.mean(values * values, axis=-1, keepdims=True))
    return (values * lax.rsqrt(power + 1e-06) * gain.astype(jnp.float32)).astype(jnp.bfloat16)

def reference(hidden_in, norm_gain, w_query, bias_query, w_key, w_value, bias_value, w_out, visible_end):
    scale = 1.0 / HEAD ** 0.5
    group = HEADS // KV
    width = HEADS * HEAD // N_TENSOR

    def section(items):
        rows, gain, wq, bq, wk, wv, bv, wo, ends = items
        normed = normalize(rows, gain)
        query = (jnp.dot(normed, wq, preferred_element_type=jnp.float32) + bq.astype(jnp.float32)).astype(jnp.bfloat16)
        keys = jnp.dot(normed, wk, preferred_element_type=jnp.float32).astype(jnp.bfloat16)
        values = (jnp.dot(normed, wv, preferred_element_type=jnp.float32) + bv.astype(jnp.float32)).astype(jnp.bfloat16)
        query_heads = query.reshape(TOKENS, HEADS, HEAD).transpose(1, 0, 2)
        key_heads = jnp.repeat(keys.reshape(TOKENS, KV, HEAD).transpose(1, 0, 2), group, axis=0)
        value_heads = jnp.repeat(values.reshape(TOKENS, KV, HEAD).transpose(1, 0, 2), group, axis=0)
        visible = jnp.arange(TOKENS, dtype=jnp.int32)[None, :] < ends[:, None]

        def head(parts):
            qq, kk, vv = parts
            scores = jnp.dot(qq, kk.T, preferred_element_type=jnp.float32) * scale
            scores = jnp.where(visible, scores, -1e+30)
            top = lax.optimization_barrier(jnp.max(scores, axis=-1, keepdims=True))
            expo = jnp.exp(scores - top)
            weights = (expo / lax.optimization_barrier(jnp.sum(expo, axis=-1, keepdims=True))).astype(jnp.bfloat16)
            return jnp.dot(weights, vv, preferred_element_type=jnp.float32).astype(jnp.bfloat16)
        context = lax.map(head, (query_heads, key_heads, value_heads))
        context = context.transpose(1, 0, 2).reshape(TOKENS, HEADS * HEAD)
        context_groups = context.reshape(TOKENS, N_TENSOR, width).transpose(1, 0, 2)
        out_groups = wo.reshape(N_TENSOR, width, D)

        def accumulate(total, parts):
            term = jnp.dot(parts[0], parts[1], preferred_element_type=jnp.float32).astype(jnp.bfloat16)
            term = lax.optimization_barrier(term)
            return (total + term.astype(jnp.float32), None)
        attended, unused = lax.scan(accumulate, jnp.zeros((TOKENS, D), jnp.float32), (context_groups, out_groups))
        return (rows.astype(jnp.float32) + attended).astype(jnp.bfloat16)
    outputs = lax.map(section, (hidden_in, norm_gain, w_query, bias_query, w_key, w_value, bias_value, w_out, visible_end))
    return jnp.roll(outputs, 1, axis=0)
```

```python
import jax
import jax.numpy as jnp
from jax import lax
from jax.experimental import pallas as pl
from jax.experimental.pallas import tpu as pltpu
from jax.sharding import PartitionSpec as P

MESH = pl.DeviceIdType.MESH
BF = jnp.bfloat16
F32 = jnp.float32
HEAD = 128
AHEAD = 3
SKEW = 2
GATHER_ACROSS = 3
LOG2E = 1.4426950408889634


def across(chunk):
    return lax.rem(chunk, 8) == 5


def mo(value, by):
    return pl.multiple_of(value, by)


def layer(
    hid, gain, wq, bq, wk, wv, bv, wo, ends, out,
    G, WQ, WKV, WO, ACC, ACCKV, Q, KV, CTX, BQ, E, KID, STG,
    ag_s, ag_r, rs_s, rs_r, ho_s, ho_r, kvw_s, kvw_r, own_kv, fw_s, fw_r,
    wq_l, wq_s, wq_r, wo_l, wo_s, wo_r, bq_s, bq_r, kv_s, kv_r, free,
):
    section = lax.axis_index("section")
    place = lax.axis_index("tensor")
    y, h, c = lax.div(place, 4), lax.rem(lax.div(place, 2), 2), lax.rem(place, 2)
    chip = lax.div(place, 2)

    def block(dy, flip):
        return lax.rem(y + dy, 4) * 2 + (1 - h if flip else h)

    def peer(dy, flip):
        return block(dy, flip) * 2 + c

    yp, ym, xx = peer(1, 0), peer(3, 0), peer(0, 1)
    other = chip * 2 + (1 - c)
    own = chip
    nxt, prv = lax.rem(section + 1, 8), lax.rem(section + 7, 8)

    def send(src, dst, ss, rs, to):
        return pltpu.make_async_remote_copy(
            src_ref=src, dst_ref=dst, send_sem=ss, recv_sem=rs,
            device_id={"tensor": to}, device_id_type=MESH,
        )

    def wq_local(j):
        return pltpu.make_async_copy(
            wq.at[0, pl.ds(mo(j * 1024, 1024), 1024), :],
            WQ.at[j, :, pl.ds(mo(c * 512, 512), 512)],
            wq_l.at[j],
        )

    def wo_local(q):
        return pltpu.make_async_copy(
            wo.at[0, :, pl.ds(mo(q * 2048, 2048), 2048)],
            WO.at[q, pl.ds(mo(c * 512, 512), 512), :],
            wo_l.at[q],
        )

    def kv_local(w, n):
        return pltpu.make_async_copy(
            w.at[0, :, pl.ds(mo(chip * HEAD, HEAD), HEAD)],
            WKV.at[chip, pl.ds(mo(c * 512, 512), 512), n * HEAD : (n + 1) * HEAD],
            own_kv.at[n],
        )

    def wq_push(j):
        return send(
            wq.at[0, pl.ds(mo(j * 1024, 1024), 1024), :],
            WQ.at[j, :, pl.ds(mo(c * 512, 512), 512)],
            wq_s.at[j], wq_r.at[j], other,
        )

    def wo_push(q):
        return send(
            wo.at[0, :, pl.ds(mo(q * 2048, 2048), 2048)],
            WO.at[q, pl.ds(mo(c * 512, 512), 512), :],
            wo_s.at[q], wo_r.at[q], other,
        )

    def kvw(w, n, d):
        to = lax.rem(chip + d, 8)
        return send(
            w.at[0, :, pl.ds(mo(to * HEAD, HEAD), HEAD)],
            WKV.at[chip, pl.ds(mo(c * 512, 512), 512), n * HEAD : (n + 1) * HEAD],
            kvw_s.at[n, d], kvw_r.at[n, d], to * 2 + c,
        )

    def forward(d):
        came = lax.rem(chip + 8 - d, 8)
        part = WKV.at[came, pl.ds(mo(c * 512, 512), 512), :]
        return send(part, part, fw_s.at[d], fw_r.at[d], other)

    def gather(kind, j):
        side = j == GATHER_ACROSS
        if kind == 0:
            b, lo, n, to = own, 0, 64, yp
        elif kind == 1:
            b, lo, n, to = own, 0, 64, ym
        elif kind == 2:
            b, lo, n, to = own, 0, 64, xx
        elif kind == 3:
            b, lo, n = jnp.where(side, block(3, 0), block(0, 1)), 0, 64
            to = jnp.where(side, xx, yp)
        elif kind == 4:
            b, lo, n = jnp.where(side, block(1, 0), block(0, 1)), 0, 64
            to = jnp.where(side, xx, ym)
        elif kind == 5:
            b, lo, n, to = block(3, 0), 0, 32, yp
        elif kind == 6:
            b, lo, n, to = block(1, 0), 32, 32, ym
        else:
            b, lo, n, to = block(2, 0), 0, 64, xx
        part = G.at[j, pl.ds(mo(b * 64 + lo, 32), n), :]
        return send(part, part, ag_s.at[kind, j], ag_r.at[kind, j], to)

    def gathered(kind, j):
        b = (block(3, 0), block(1, 0), block(0, 1), block(3, 1), block(1, 1),
             block(2, 0), block(2, 0), block(2, 1))[kind]
        lo = 32 if kind == 6 else 0
        n = 32 if kind in (5, 6) else 64
        part = G.at[j, pl.ds(mo(b * 64 + lo, 32), n), :]
        send(part, part, ag_s.at[kind, j], ag_r.at[kind, j], xx).wait_recv()

    def term(k, b, half=0):
        return lax.div(k, 4), mo(lax.rem(k, 4) * 256 + b * 32 + half * 16, 16)

    def slot(k, n, half=0):
        return lax.div(k, 2), mo(lax.rem(k, 2) * 256 + n * 32 + half * 16, 16)

    def reduce(kind, k):
        side = across(k)
        half, rows, into, at = 0, 32, kind, 0
        if kind == 0:
            b, to = block(3, 0), ym
        elif kind == 1:
            b, to = block(1, 0), yp
        elif kind == 2:
            b, to = block(0, 1), xx
        elif kind == 3:
            b, to = block(3, 1), jnp.where(side, xx, ym)
        elif kind == 4:
            b, to = block(1, 1), jnp.where(side, xx, yp)
        elif kind == 5:
            b, to, rows = block(2, 0), ym, 16
        elif kind == 6:
            b, to, rows, half, into, at = block(2, 0), yp, 16, 1, 5, 1
        else:
            b, to, into = block(2, 1), xx, 6
        i, row = term(k, b, half)
        o, line = slot(k, into, at)
        return send(
            WQ.at[i, pl.ds(row, rows), :], G.at[o, pl.ds(line, rows), :],
            rs_s.at[kind, k], rs_r.at[kind, k], to,
        )

    def add(k, b, half, arrived):
        i, row = term(k, b, half)
        total = WQ[i, pl.ds(row, 16), :].astype(F32)
        for n, at in arrived:
            o, line = slot(k, n, at)
            total = total + G[o, pl.ds(line, 16), :].astype(F32)
        return total, i, row

    def add_in(k, b, half, arrived):
        total, i, row = add(k, b, half, arrived)
        WQ[i, pl.ds(row, 16), :] = total.astype(BF)

    def hand(k):
        r, q = lax.div(k, 4), lax.rem(k, 4)
        rows, columns = pl.ds(mo(r * 16, 16), 16), pl.ds(mo(q * 2048, 2048), 2048)
        return pltpu.make_async_remote_copy(
            src_ref=STG.at[rows, columns], dst_ref=out.at[0, rows, columns],
            send_sem=ho_s.at[k], recv_sem=ho_r.at[k],
            device_id={"section": nxt}, device_id_type=MESH,
        )

    for n, w in enumerate((wk, wv)):
        kv_local(w, n).start()
    for j in range(8):
        wq_local(j).start()
    for q in range(4):
        wo_local(q).start()

    barrier = pltpu.get_barrier_semaphore()
    for d in range(1, 8):
        pl.semaphore_signal(
            barrier, inc=1, device_id={"tensor": lax.rem(chip + d, 8) * 2 + c}, device_id_type=MESH
        )
    pl.semaphore_signal(barrier, inc=1, device_id={"tensor": other}, device_id_type=MESH)
    pl.semaphore_signal(barrier, inc=1, device_id={"section": prv}, device_id_type=MESH)
    pl.semaphore_wait(barrier, 9)

    for d in (4, 3, 5, 2, 6, 1, 7):
        for n, w in enumerate((wk, wv)):
            kvw(w, n, d).start()

    def norm_rows(rg, carry):
        rows = hid[0, pl.ds(mo(rg * 16, 16), 16), :].astype(F32)
        power = jnp.mean(rows * rows, axis=-1, keepdims=True)
        scale = lax.rsqrt(power + 1e-06)
        normed = (rows * scale * gain[...].astype(F32)).astype(BF)
        for j in range(8):
            G[j, pl.ds(mo(own * 64 + rg * 16, 16), 16), :] = normed[:, j * 1024 : (j + 1) * 1024]
        return carry

    lax.fori_loop(0, 4, norm_rows, 0)
    for j in range(AHEAD):
        for kind in range(3):
            gather(kind, j).start()
    BQ[c] = jnp.broadcast_to(bq[...], (16, 512))
    bias_push = send(BQ.at[c], BQ.at[c], bq_s.at[0], bq_r.at[0], other)
    bias_push.start()
    for j in range(8):
        wq_push(j).start()
    for q in range(4):
        wo_push(q).start()
    ACC[...] = jnp.zeros_like(ACC)
    ACCKV[...] = jnp.zeros_like(ACCKV)
    for b in range(8):
        line = jnp.broadcast_to(ends[:, b * 128 : (b + 1) * 128].astype(F32), (128, 128))
        E[b] = line.T
    lane = lax.broadcasted_iota(jnp.int32, (8, 512), 1)
    token = lane + lax.div(lane, 64) * 64
    KID[:, 0:512] = token.astype(F32)
    KID[:, 512:1024] = (token + 64).astype(F32)
    KV[:, 256:384] = jnp.ones((1024, 128), BF)

    def kv_stage(j, carry):
        ACCKV[...] += jnp.dot(G[j], WKV[j], preferred_element_type=F32)
        return carry

    def gather_step(i, carry):
        @pl.when(i < 8 - AHEAD)
        def _():
            for kind in range(3):
                gather(kind, i + AHEAD).start()

        @pl.when(i < 8)
        def _():
            gathered(0, i)
            gather(5, i).start()
            gathered(1, i)
            gather(6, i).start()
            gathered(2, i)
            gather(3, i).start()
            gather(4, i).start()

        @pl.when(i == 0)
        def _():
            for n, w in enumerate((wk, wv)):
                kv_local(w, n).wait()
            forward(0).start()

        @pl.when((i >= 1) & (i < 8))
        def _():
            for n, w in enumerate((wk, wv)):
                came = lax.rem(chip + 8 - i, 8)
                part = WKV.at[came, pl.ds(mo(c * 512, 512), 512), n * HEAD : (n + 1) * HEAD]
                send(part, part, kvw_s.at[n, i], kvw_r.at[n, i], other).wait_recv()
            forward(i).start()

        @pl.when((i >= 1) & (i < 9))
        def _():
            gathered(5, i - 1)
            gathered(6, i - 1)
            gather(7, i - 1).start()

        @pl.when(i >= 3)
        def _():
            j = i - 3
            gathered(3, j)
            gathered(4, j)
            gathered(7, j)

            @pl.when(i == 8)
            def _():
                for d in range(8):
                    came = lax.rem(chip + 8 - d, 8)
                    part = WKV.at[came, pl.ds(mo((1 - c) * 512, 512), 512), :]
                    send(part, part, fw_s.at[d], fw_r.at[d], other).wait_recv()

            @pl.when(i >= 8)
            def _():
                lax.fori_loop((i - 8) * 3, jnp.minimum((i - 8) * 3 + 3, 8), kv_stage, 0)

            @pl.when(i == 10)
            def _():
                total = ACCKV[...]
                rows = pl.ds(mo(c * 512, 512), 512)
                KV[rows, 0:HEAD] = total[:, 0:HEAD].astype(BF)
                bias = bv[:, pl.ds(mo(chip * HEAD, HEAD), HEAD)].astype(F32)
                KV[rows, HEAD : 2 * HEAD] = (total[:, HEAD:] + bias).astype(BF)
                part = KV.at[rows, 0 : 2 * HEAD]
                send(part, part, kv_s.at[0], kv_r.at[0], other).start()

            wq_local(j).wait()
            part = WQ.at[j, :, pl.ds(mo((1 - c) * 512, 512), 512)]
            send(part, part, wq_s.at[j], wq_r.at[j], other).wait_recv()
            for n in range(2):
                columns = slice(n * 512, (n + 1) * 512)
                ACC[:, columns] += jnp.dot(G[j], WQ[j, :, columns], preferred_element_type=F32)

        return carry

    lax.fori_loop(0, 11, gather_step, 0)

    send(BQ.at[1 - c], BQ.at[1 - c], bq_s.at[0], bq_r.at[0], other).wait_recv()
    for n in range(2):
        for b in range(8):
            Q[b, :, n * 512 : (n + 1) * 512] = (
                ACC[b * 64 : (b + 1) * 64, n * 512 : (n + 1) * 512] + BQ[n, 0:1, :].astype(F32)
            ).astype(BF)

    def gather_sent(j, carry):
        for kind in range(8):
            gather(kind, j).wait_send()
        return carry

    lax.fori_loop(0, 8, gather_sent, 0)
    for to in (yp, ym, xx):
        pl.semaphore_signal(free, inc=1, device_id={"tensor": to}, device_id_type=MESH)

    part = KV.at[pl.ds(mo((1 - c) * 512, 512), 512), 0 : 2 * HEAD]
    send(part, part, kv_s.at[0], kv_r.at[0], other).wait_recv()

    def attend(r, head):
        rows, columns = pl.ds(mo(r * 16, 16), 16), pl.ds(mo(head * HEAD, HEAD), HEAD)
        query = Q[:, rows, columns].reshape(128, HEAD)
        scores = lax.dot_general(
            query, KV[:, 0:HEAD], (((1,), (1,)), ((), ())), preferred_element_type=F32
        )
        end = E[:, pl.ds(mo(c * 64 + r * 16, 16), 16), 0:1].reshape(128, 1)
        scores = jnp.where(KID[0:1, :] < end, scores, -1e30 * HEAD**0.5)
        top = jnp.max(scores, axis=-1, keepdims=True)
        expo = jnp.exp2((scores - top) * (LOG2E / HEAD**0.5)).astype(BF)
        mixed = jnp.dot(expo, KV[:, HEAD : 3 * HEAD], preferred_element_type=F32)
        CTX[lax.rem(r, 2), :, columns] = (mixed[:, :HEAD] / mixed[:, HEAD:]).astype(BF)

    def attend_first(head, carry):
        attend(0, head)
        return carry

    lax.fori_loop(0, 8, attend_first, 0)
    pl.semaphore_wait(free, 3)
    for q in range(4):
        wo_local(q).wait()
        part = WO.at[q, pl.ds(mo((1 - c) * 512, 512), 512), :]
        send(part, part, wo_s.at[q], wo_r.at[q], other).wait_recv()

    def arrived(kind, k):
        into, at = {6: (5, 1), 7: (6, 0)}.get(kind, (kind, 0))
        o, line = slot(k, into, at)
        part = G.at[o, pl.ds(line, 16 if kind in (5, 6) else 32), :]
        send(part, part, rs_s.at[kind, k], rs_r.at[kind, k], xx).wait_recv()

    def reduce_step(i, carry):
        k1, k2, k3 = i - SKEW, i - 2 * SKEW, i - 3 * SKEW

        @pl.when(i < 16)
        def _():
            r, q = lax.div(i, 4), lax.rem(i, 4)
            for half in range(2):
                terms = jnp.dot(
                    CTX[lax.rem(r, 2)],
                    WO[q, :, half * 1024 : (half + 1) * 1024],
                    preferred_element_type=F32,
                ).astype(BF)
                for b in range(8):
                    n, row = term(i, b, half)
                    WQ[n, pl.ds(row, 16), :] = terms[b * 16 : (b + 1) * 16]
            reduce(7, i).start()
            reduce(3, i).start()
            reduce(4, i).start()

        @pl.when((k1 >= 0) & (k1 < 16))
        def _():
            arrived(7, k1)
            for half in range(2):
                add_in(k1, block(2, 0), half, [(6, half)])
                reduce(5 + half, k1).start()

            @pl.when(jnp.logical_not(across(k1)))
            def _():
                arrived(3, k1)
                arrived(4, k1)
                for half in range(2):
                    add_in(k1, block(0, 1), half, [(3, half), (4, half)])

            reduce(2, k1).start()

        @pl.when((k2 >= 0) & (k2 < 16))
        def _():
            arrived(5, k2)
            add_in(k2, block(3, 0), 0, [(5, 0)])
            arrived(6, k2)
            add_in(k2, block(1, 0), 1, [(5, 1)])

            @pl.when(across(k2))
            def _():
                arrived(3, k2)
                arrived(4, k2)
                for half in range(2):
                    add_in(k2, block(3, 0), half, [(3, half)])
                    add_in(k2, block(1, 0), half, [(4, half)])

            reduce(0, k2).start()
            reduce(1, k2).start()

        @pl.when(k3 >= 0)
        def _():
            for kind in range(3):
                arrived(kind, k3)
            r, q = lax.div(k3, 4), lax.rem(k3, 4)
            rows = pl.ds(mo(r * 16, 16), 16)
            for half in range(2):
                total, _, _ = add(k3, own, half, [(0, half), (1, half), (2, half)])
                columns = pl.ds(mo(q * 2048 + half * 1024, 1024), 1024)
                STG[rows, columns] = (hid[0, rows, columns].astype(F32) + total).astype(BF)
            hand(k3).start()

        @pl.when(i < 12)
        def _():
            for n in range(2):
                attend(lax.div(i, 4) + 1, lax.rem(i, 4) * 2 + n)

        return carry

    lax.fori_loop(0, 16 + 3 * SKEW, reduce_step, 0)

    def sent(k, carry):
        for kind in range(8):
            reduce(kind, k).wait_send()
        hand(k).wait()
        return carry

    lax.fori_loop(0, 16, sent, 0)
    for d in range(1, 8):
        for n, w in enumerate((wk, wv)):
            kvw(w, n, d).wait_send()
    for d in range(8):
        forward(d).wait_send()
    for j in range(8):
        wq_push(j).wait_send()
    for q in range(4):
        wo_push(q).wait_send()
    bias_push.wait_send()
    part = KV.at[pl.ds(mo(c * 512, 512), 512), 0 : 2 * HEAD]
    send(part, part, kv_s.at[0], kv_r.at[0], other).wait_send()


def on_device(
    hidden_in, norm_gain, w_query, bias_query, w_key, w_value, bias_value, w_out, visible_end
):
    vmem, anywhere = pl.BlockSpec(memory_space=pltpu.VMEM), pl.BlockSpec(memory_space=pl.ANY)
    dma = pltpu.SemaphoreType.DMA
    return pl.pallas_call(
        layer,
        out_shape=jax.ShapeDtypeStruct(hidden_in.shape, BF),
        in_specs=[vmem, vmem, anywhere, vmem, anywhere, anywhere, vmem, anywhere, vmem],
        out_specs=anywhere,
        scratch_shapes=[
            pltpu.VMEM((8, 512, 1024), BF),
            pltpu.VMEM((8, 1024, 1024), BF),
            pltpu.VMEM((8, 1024, 256), BF),
            pltpu.VMEM((4, 1024, 2048), BF),
            pltpu.VMEM((512, 1024), F32),
            pltpu.VMEM((512, 256), F32),
            pltpu.VMEM((8, 64, 1024), BF),
            pltpu.VMEM((1024, 384), BF),
            pltpu.VMEM((2, 128, 1024), BF),
            pltpu.VMEM((2, 16, 512), BF),
            pltpu.VMEM((8, 128, 128), F32),
            pltpu.VMEM((8, 1024), F32),
            pltpu.VMEM((64, 8192), BF),
            dma((8, 8)), dma((8, 8)), dma((8, 16)), dma((8, 16)), dma((16,)), dma((16,)),
            dma((2, 8)), dma((2, 8)), dma((2,)), dma((8,)), dma((8,)),
            dma((8,)), dma((8,)), dma((8,)), dma((4,)), dma((4,)), dma((4,)),
            dma((1,)), dma((1,)), dma((1,)), dma((1,)), pltpu.SemaphoreType.REGULAR,
        ],
        compiler_params=pltpu.CompilerParams(
            collective_id=0, has_side_effects=True, vmem_limit_bytes=63 * 2**20
        ),
        cost_estimate=pl.CostEstimate(flops=24 * 10**9, bytes_accessed=40 * 10**6, transcendentals=4 * 2**20),
    )(
        hidden_in, norm_gain, w_query, bias_query, w_key, w_value, bias_value, w_out, visible_end
    )


def solution(mesh):
    placed = (
        P("section", "tensor", None),
        P("section", None),
        P("section", None, "tensor"),
        P("section", "tensor"),
        P("section", "tensor", None),
        P("section", "tensor", None),
        P("section", None),
        P("section", "tensor", None),
        P("section", None),
    )
    return jax.shard_map(
        on_device,
        mesh=mesh,
        in_specs=placed,
        out_specs=P("section", "tensor", None),
        check_vma=False,
    )
```

```python
import jax
import jax.numpy as jnp
from jax import lax
from jax.experimental import pallas as pl
from jax.experimental.pallas import tpu as pltpu
from jax.sharding import PartitionSpec as P

MESH = pl.DeviceIdType.MESH
BF = jnp.bfloat16
F32 = jnp.float32
HEAD = 128
RELAYED = 4
UP_FRONT = 4
KV_STEPS = (2, 5, 4)
LOG2E = 1.4426950408889634


def mo(value, by):
    return pl.multiple_of(value, by)


def layer(
    hid, gain, wq, bq, wk, wv, bv, wo, ends, out,
    G, WQ, WKV, WO, ACC, KVT, KVIN, Q, KV, CTX, BQ, E, KID, STG, RELAY,
    ag_s, ag_r, rs_s, rs_r, ho_s, ho_r, rl_s, rl_r, wkv_l, wkv_s, wkv_r, kvt_s, kvt_r,
    wq_l, wq_s, wq_r, wo_l, wo_s, wo_r, bq_s, bq_r, kv_s, kv_r, free,
):
    section = lax.axis_index("section")
    place = lax.axis_index("tensor")
    y, h, c = lax.div(place, 4), lax.rem(lax.div(place, 2), 2), lax.rem(place, 2)
    chip = lax.div(place, 2)

    def block(dy, flip):
        return lax.rem(y + dy, 4) * 2 + (1 - h if flip else h)

    def peer(dy, flip):
        return block(dy, flip) * 2 + c

    yp, ym, xx = peer(1, 0), peer(3, 0), peer(0, 1)
    other = chip * 2 + (1 - c)
    own = chip
    nxt, prv = lax.rem(section + 1, 8), lax.rem(section + 7, 8)
    half, z = lax.div(section, 4), lax.rem(section, 4)
    first, last = z == 0, z == 3

    def send(src, dst, ss, rs, to):
        return pltpu.make_async_remote_copy(
            src_ref=src, dst_ref=dst, send_sem=ss, recv_sem=rs,
            device_id={"tensor": to}, device_id_type=MESH,
        )

    def wq_local(j):
        return pltpu.make_async_copy(
            wq.at[0, pl.ds(mo(j * 1024, 1024), 1024), :],
            WQ.at[j, :, pl.ds(mo(c * 512, 512), 512)],
            wq_l.at[j],
        )

    def wo_local(q):
        return pltpu.make_async_copy(
            wo.at[0, :, pl.ds(mo(q * 1024, 1024), 1024)],
            WO.at[q, pl.ds(mo(c * 512, 512), 512), :],
            wo_l.at[q],
        )

    def kv_local(w, n):
        return pltpu.make_async_copy(
            w.at[0], WKV.at[n, pl.ds(mo(c * 512, 512), 512), :], wkv_l.at[n]
        )

    def kv_push(w, n):
        there = WKV.at[n, pl.ds(mo(c * 512, 512), 512), :]
        return send(w.at[0], there, wkv_s.at[n], wkv_r.at[n], other)

    def wq_push(j):
        return send(
            wq.at[0, pl.ds(mo(j * 1024, 1024), 1024), :],
            WQ.at[j, :, pl.ds(mo(c * 512, 512), 512)],
            wq_s.at[j], wq_r.at[j], other,
        )

    def wo_push(q):
        return send(
            wo.at[0, :, pl.ds(mo(q * 1024, 1024), 1024)],
            WO.at[q, pl.ds(mo(c * 512, 512), 512), :],
            wo_s.at[q], wo_r.at[q], other,
        )

    def piece(b, j, lo=0, n=64):
        return G.at[j, pl.ds(mo(b * 64 + lo, 32), n), :]

    def gather(kind, j):
        b = (own, own, own, block(0, 1), block(0, 1), block(3, 0), block(1, 0), block(2, 0))[kind]
        to = (yp, ym, xx, yp, ym, yp, ym, xx)[kind]
        part = piece(b, j, 32 if kind == 6 else 0, 32 if kind in (5, 6) else 64)
        return send(part, part, ag_s.at[kind, j], ag_r.at[kind, j], to)

    def gather_side(kind):
        b = block(3, 0) if kind == 3 else block(1, 0)
        part = piece(b, b)
        return send(part, part, ag_s.at[kind, block(0, 1)], ag_r.at[kind, b], xx)

    def gathered(kind, j):
        b = (block(3, 0), block(1, 0), block(0, 1), block(3, 1), block(1, 1),
             block(2, 0), block(2, 0), block(2, 1))[kind]
        part = piece(b, j, 32 if kind == 6 else 0, 32 if kind in (5, 6) else 64)
        send(part, part, ag_s.at[kind, j], ag_r.at[kind, j], xx).wait_recv()

    def kv_sum(kind):
        b = (block(3, 0), block(1, 0), block(0, 1), block(3, 1), block(1, 1),
             block(2, 0), block(2, 0), block(2, 1))[kind]
        lo, n = (256 if kind == 6 else 0), (256 if kind in (5, 6) else 512)
        to = (ym, yp, xx, ym, yp, ym, yp, xx)[kind]
        into = (0, 1, 2, 3, 4, 5, 5, 6)[kind]
        return send(
            KVT.at[b, lo : lo + n, :], KVIN.at[into, lo : lo + n, :],
            kvt_s.at[kind], kvt_r.at[kind], to,
        )

    def kv_came(kind):
        lo, n = (256 if kind == 6 else 0), (256 if kind in (5, 6) else 512)
        into = (0, 1, 2, 3, 4, 5, 5, 6)[kind]
        part = KVIN.at[into, lo : lo + n, :]
        send(part, part, kvt_s.at[kind], kvt_r.at[kind], xx).wait_recv()
        return KVIN[into, lo : lo + n, :].astype(F32)

    order = (
        block(2, 1), block(1, 1), block(3, 1), block(2, 0), block(0, 1), block(1, 0), block(3, 0), own,
    )

    def reduce(kind, k):
        at, n = (384, 320, 256, 128, 64, 192, 224, 0)[kind], 32 if kind in (5, 6) else 64
        line = (0, 64, 128, 192, 256, 320, 352, 384)[kind]
        to = (ym, yp, xx, ym, yp, ym, yp, xx)[kind]
        return send(
            WQ.at[k, at : at + n, :], G.at[k, line : line + n, :],
            rs_s.at[kind, k], rs_r.at[kind, k], to,
        )

    def arrived(kind, k):
        n = 32 if kind in (5, 6) else 64
        line = (0, 64, 128, 192, 256, 320, 352, 384)[kind]
        part = G.at[k, line : line + n, :]
        send(part, part, rs_s.at[kind, k], rs_r.at[kind, k], xx).wait_recv()
        return G[k, line : line + n, :].astype(F32)

    def term(k, at, n=64):
        return WQ[k, at : at + n, :].astype(F32)

    def hand_to(src, dst, ss, rs, to):
        return pltpu.make_async_remote_copy(
            src_ref=src, dst_ref=dst, send_sem=ss, recv_sem=rs,
            device_id={"section": to}, device_id_type=MESH,
        )

    def hand(k):
        columns = pl.ds(mo(k * 1024, 1024), 1024)
        return hand_to(STG.at[:, columns], out.at[0, :, columns], ho_s.at[k], ho_r.at[k], nxt)

    def relay_in(k):
        columns = pl.ds(mo(k * 1024, 1024), 1024)
        return hand_to(STG.at[:, columns], RELAY.at[k], ho_s.at[k], rl_r.at[k], half * 4)

    def relay_out(k):
        columns = pl.ds(mo(k * 1024, 1024), 1024)
        to = (1 - half) * 4
        return hand_to(RELAY.at[k], out.at[0, :, columns], rl_s.at[k], ho_r.at[k], to)

    for n, w in enumerate((wk, wv)):
        kv_local(w, n).start()
    for j in range(8):
        wq_local(j).start()
    for q in range(8):
        wo_local(q).start()

    barrier = pltpu.get_barrier_semaphore()
    for to in (yp, ym, xx, other):
        pl.semaphore_signal(barrier, inc=1, device_id={"tensor": to}, device_id_type=MESH)
    pl.semaphore_signal(barrier, inc=1, device_id={"section": prv}, device_id_type=MESH)

    @pl.when(first)
    def _():
        for to in (half * 4 + 3, (1 - half) * 4):
            pl.semaphore_signal(barrier, inc=1, device_id={"section": to}, device_id_type=MESH)

    @pl.when(first | last)
    def _():
        pl.semaphore_wait(barrier, 6)

    @pl.when(jnp.logical_not(first | last))
    def _():
        pl.semaphore_wait(barrier, 5)


    for n, w in enumerate((wk, wv)):
        kv_push(w, n).start()

    def norm_rows(rg, carry):
        rows = hid[0, pl.ds(mo(rg * 16, 16), 16), :].astype(F32)
        power = jnp.mean(rows * rows, axis=-1, keepdims=True)
        scale = lax.rsqrt(power + 1e-06)
        normed = (rows * scale * gain[...].astype(F32)).astype(BF)
        for j in range(8):
            G[j, pl.ds(mo(own * 64 + rg * 16, 16), 16), :] = normed[:, j * 1024 : (j + 1) * 1024]
        return carry

    lax.fori_loop(0, 4, norm_rows, 0)
    rest = [block(0, 0), block(0, 1), block(1, 1), block(3, 1)]
    own_order = (
        [block(1, 0), block(2, 0), block(2, 1), block(3, 0), *rest],
        [block(3, 0), block(2, 0), block(2, 1), block(1, 0), *rest],
        [block(0, 1), block(1, 1), block(3, 1), block(2, 1), block(0, 0), block(1, 0), block(2, 0), block(3, 0)],
    )
    for n in range(UP_FRONT):
        for kind in range(3):
            gather(kind, own_order[kind][n]).start()
    BQ[c] = jnp.broadcast_to(bq[...], (16, 512))
    bias_push = send(BQ.at[c], BQ.at[c], bq_s.at[0], bq_r.at[0], other)
    bias_push.start()
    for j in range(8):
        wq_push(j).start()
    for q in range(8):
        wo_push(q).start()
    ACC[...] = jnp.zeros_like(ACC)
    for b in range(8):
        line = jnp.broadcast_to(ends[:, b * 128 : (b + 1) * 128].astype(F32), (128, 128))
        E[b] = line.T
    lane = lax.broadcasted_iota(jnp.int32, (8, 512), 1)
    token = lane + lax.div(lane, 64) * 64
    KID[:, 0:512] = token.astype(F32)
    KID[:, 512:1024] = (token + 64).astype(F32)
    KV[:, 256:384] = jnp.ones((1024, 128), BF)

    gathered(0, block(1, 0))
    gather(5, block(1, 0)).start()
    gathered(1, block(3, 0))
    gather(6, block(3, 0)).start()
    gathered(2, block(1, 0))
    gather(3, block(1, 0)).start()
    gathered(2, block(3, 0))
    gather(4, block(3, 0)).start()
    gathered(0, block(1, 1))
    gather(5, block(1, 1)).start()
    gathered(1, block(3, 1))
    gather(6, block(3, 1)).start()
    for n in range(UP_FRONT, 8):
        for kind in range(3):
            gather(kind, own_order[kind][n]).start()
    gathered(5, block(0, 1))
    gathered(6, block(0, 1))
    gather(7, block(0, 1)).start()
    gathered(0, own)
    gather(5, own).start()
    gathered(1, own)
    gather(6, own).start()
    for kind in range(2, 8):
        gathered(kind, own)

    for n, w in enumerate((wk, wv)):
        kv_local(w, n).wait()
        part = WKV.at[n, pl.ds(mo((1 - c) * 512, 512), 512), :]
        send(part, part, wkv_s.at[n], wkv_r.at[n], other).wait_recv()
        for m in range(2):
            sums = jnp.dot(
                G[own], WKV[n, :, m * 512 : (m + 1) * 512], preferred_element_type=F32
            ).astype(BF)
            for b in range(4):
                KVT[m * 4 + b, :, n * HEAD : (n + 1) * HEAD] = sums[:, b * HEAD : (b + 1) * HEAD]
    for kind in (7, 3, 4):
        kv_sum(kind).start()

    def pass_along(j, carry):
        @pl.when((j != block(1, 0)) & (j != block(1, 1)) & (j != own))
        def _():
            gathered(0, j)
            gather(5, j).start()

        @pl.when((j != block(3, 0)) & (j != block(3, 1)) & (j != own))
        def _():
            gathered(1, j)
            gather(6, j).start()

        return carry

    lax.fori_loop(0, 8, pass_along, 0)
    gather_side(3).start()
    gather_side(4).start()

    def pass_across(j, carry):
        @pl.when((j != block(1, 0)) & (j != block(3, 0)) & (j != own))
        def _():
            gathered(2, j)

        @pl.when((j != block(1, 0)) & (j != block(0, 1)))
        def _():
            gather(3, j).start()

        @pl.when((j != block(3, 0)) & (j != block(0, 1)))
        def _():
            gather(4, j).start()

        @pl.when(j != block(0, 1))
        def _():
            @pl.when(j != own)
            def _():
                gathered(5, j)
                gathered(6, j)

            gather(7, j).start()

        @pl.when(j == KV_STEPS[0])
        def _():
            b = block(2, 0)
            KVT[b] = (KVT[b].astype(F32) + kv_came(7)).astype(BF)
            kv_sum(5).start()
            kv_sum(6).start()
            b = block(0, 1)
            KVT[b] = (KVT[b].astype(F32) + kv_came(3) + kv_came(4)).astype(BF)
            kv_sum(2).start()

        @pl.when(j == KV_STEPS[1])
        def _():
            b = block(3, 0)
            KVT[b, 0:256, :] = (KVT[b, 0:256, :].astype(F32) + kv_came(5)).astype(BF)
            kv_sum(0).start()
            b = block(1, 0)
            KVT[b, 256:512, :] = (KVT[b, 256:512, :].astype(F32) + kv_came(6)).astype(BF)
            kv_sum(1).start()

        return carry

    lax.fori_loop(0, 8, pass_across, 0)

    def project(j, carry):
        wq_local(j).wait()
        part = WQ.at[j, :, pl.ds(mo((1 - c) * 512, 512), 512)]
        send(part, part, wq_s.at[j], wq_r.at[j], other).wait_recv()

        @pl.when(j != own)
        def _():
            gathered(3, j)
            gathered(4, j)
            gathered(7, j)

        for n in range(2):
            columns = slice(n * 512, (n + 1) * 512)
            ACC[:, columns] += jnp.dot(G[j], WQ[j, :, columns], preferred_element_type=F32)

        @pl.when(j == KV_STEPS[2])
        def _():
            total = KVT[own].astype(F32) + kv_came(0) + kv_came(1) + kv_came(2)
            rows = pl.ds(mo(c * 512, 512), 512)
            KV[rows, 0:HEAD] = total[:, 0:HEAD].astype(BF)
            bias = bv[:, pl.ds(mo(chip * HEAD, HEAD), HEAD)].astype(F32)
            KV[rows, HEAD : 2 * HEAD] = (total[:, HEAD:] + bias).astype(BF)
            part = KV.at[rows, 0 : 2 * HEAD]
            send(part, part, kv_s.at[0], kv_r.at[0], other).start()

        return carry

    lax.fori_loop(0, 8, project, 0)

    send(BQ.at[1 - c], BQ.at[1 - c], bq_s.at[0], bq_r.at[0], other).wait_recv()
    for n in range(2):
        for b in range(8):
            Q[b, :, n * 512 : (n + 1) * 512] = (
                ACC[b * 64 : (b + 1) * 64, n * 512 : (n + 1) * 512] + BQ[n, 0:1, :].astype(F32)
            ).astype(BF)

    def gather_sent(j, carry):
        for kind in range(8):
            gather(kind, j).wait_send()
        return carry

    lax.fori_loop(0, 8, gather_sent, 0)
    for to in (yp, ym, xx):
        pl.semaphore_signal(free, inc=1, device_id={"tensor": to}, device_id_type=MESH)

    part = KV.at[pl.ds(mo((1 - c) * 512, 512), 512), 0 : 2 * HEAD]
    send(part, part, kv_s.at[0], kv_r.at[0], other).wait_recv()

    def attend(first, last, head):
        columns = pl.ds(mo(head * HEAD, HEAD), HEAD)
        blocks = order[first:last]
        query = jnp.concatenate([Q[b, :, columns] for b in blocks], axis=0)
        scores = lax.dot_general(
            query, KV[:, 0:HEAD], (((1,), (1,)), ((), ())), preferred_element_type=F32
        )
        end = jnp.concatenate([E[b, pl.ds(mo(c * 64, 64), 64), 0:1] for b in blocks], axis=0)
        scores = jnp.where(KID[0:1, :] < end, scores, -1e30 * HEAD**0.5)
        top = jnp.max(scores, axis=-1, keepdims=True)
        expo = jnp.exp2((scores - top) * (LOG2E / HEAD**0.5)).astype(BF)
        mixed = jnp.dot(expo, KV[:, HEAD : 3 * HEAD], preferred_element_type=F32)
        CTX[first * 64 : last * 64, columns] = (mixed[:, :HEAD] / mixed[:, HEAD:]).astype(BF)

    def terms(first, last, k):
        rows = slice(first * 64, last * 64)
        WQ[k, rows, :] = jnp.dot(CTX[rows, :], WO[k], preferred_element_type=F32).astype(BF)

    def attend_first(head, carry):
        attend(0, 3, head)
        return carry

    lax.fori_loop(0, 8, attend_first, 0)
    pl.semaphore_wait(free, 3)

    def far_terms(k, carry):
        wo_local(k).wait()
        part = WO.at[k, pl.ds(mo((1 - c) * 512, 512), 512), :]
        send(part, part, wo_s.at[k], wo_r.at[k], other).wait_recv()
        terms(0, 3, k)
        reduce(3, k).start()
        reduce(4, k).start()
        reduce(7, k).start()
        attend(3, 5, k)
        return carry

    lax.fori_loop(0, 8, far_terms, 0)

    def middle_terms(k, carry):
        terms(3, 5, k)
        WQ[k, 192:256, :] = (term(k, 192) + arrived(7, k)).astype(BF)
        reduce(5, k).start()
        reduce(6, k).start()
        WQ[k, 256:320, :] = (term(k, 256) + arrived(3, k) + arrived(4, k)).astype(BF)
        reduce(2, k).start()
        attend(5, 8, k)
        return carry

    lax.fori_loop(0, 8, middle_terms, 0)

    def near_terms(i, carry):
        @pl.when(i < 8)
        def _():
            k = i
            terms(5, 8, k)
            WQ[k, 384:416, :] = (term(k, 384, 32) + arrived(5, k)).astype(BF)
            WQ[k, 352:384, :] = (term(k, 352, 32) + arrived(6, k)).astype(BF)
            reduce(0, k).start()
            reduce(1, k).start()

        @pl.when(i >= 1)
        def _():
            k = i - 1
            columns = pl.ds(mo(k * 1024, 1024), 1024)
            total = term(k, 448) + arrived(0, k) + arrived(1, k) + arrived(2, k)
            STG[:, columns] = (hid[0, :, columns].astype(F32) + total).astype(BF)

            @pl.when(last & (k < RELAYED))
            def _():
                relay_in(k).start()

            @pl.when(jnp.logical_not(last & (k < RELAYED)))
            def _():
                hand(k).start()

        @pl.when(first & (i >= 3) & (i < 3 + RELAYED))
        def _():
            relay_in(i - 3).wait_recv()
            relay_out(i - 3).start()

        return carry

    lax.fori_loop(0, 9, near_terms, 0)

    def sent(k, carry):
        for kind in range(8):
            reduce(kind, k).wait_send()
        hand(k).wait()

        @pl.when(first & (k < RELAYED))
        def _():
            relay_out(k).wait_send()

        return carry

    lax.fori_loop(0, 8, sent, 0)
    for n, w in enumerate((wk, wv)):
        kv_push(w, n).wait_send()
    for kind in range(8):
        kv_sum(kind).wait_send()
    for j in range(8):
        wq_push(j).wait_send()
    for q in range(8):
        wo_push(q).wait_send()
    bias_push.wait_send()
    part = KV.at[pl.ds(mo(c * 512, 512), 512), 0 : 2 * HEAD]
    send(part, part, kv_s.at[0], kv_r.at[0], other).wait_send()


def on_device(
    hidden_in, norm_gain, w_query, bias_query, w_key, w_value, bias_value, w_out, visible_end
):
    vmem, anywhere = pl.BlockSpec(memory_space=pltpu.VMEM), pl.BlockSpec(memory_space=pl.ANY)
    dma = pltpu.SemaphoreType.DMA
    return pl.pallas_call(
        layer,
        out_shape=jax.ShapeDtypeStruct(hidden_in.shape, BF),
        in_specs=[vmem, vmem, anywhere, vmem, anywhere, anywhere, vmem, anywhere, vmem],
        out_specs=anywhere,
        scratch_shapes=[
            pltpu.VMEM((8, 512, 1024), BF),
            pltpu.VMEM((8, 1024, 1024), BF),
            pltpu.VMEM((2, 1024, 1024), BF),
            pltpu.VMEM((8, 1024, 1024), BF),
            pltpu.VMEM((512, 1024), F32),
            pltpu.VMEM((8, 512, 256), BF),
            pltpu.VMEM((7, 512, 256), BF),
            pltpu.VMEM((8, 64, 1024), BF),
            pltpu.VMEM((1024, 384), BF),
            pltpu.VMEM((512, 1024), BF),
            pltpu.VMEM((2, 16, 512), BF),
            pltpu.VMEM((8, 128, 128), F32),
            pltpu.VMEM((8, 1024), F32),
            pltpu.VMEM((64, 8192), BF),
            pltpu.VMEM((RELAYED, 64, 1024), BF),
            dma((8, 8)), dma((8, 8)), dma((8, 8)), dma((8, 8)), dma((8,)), dma((8,)), dma((8,)), dma((8,)),
            dma((2,)), dma((2,)), dma((2,)), dma((8,)), dma((8,)),
            dma((8,)), dma((8,)), dma((8,)), dma((8,)), dma((8,)), dma((8,)),
            dma((1,)), dma((1,)), dma((1,)), dma((1,)), pltpu.SemaphoreType.REGULAR,
        ],
        compiler_params=pltpu.CompilerParams(
            collective_id=0, has_side_effects=True, vmem_limit_bytes=63 * 2**20
        ),
        cost_estimate=pl.CostEstimate(flops=24 * 10**9, bytes_accessed=40 * 10**6, transcendentals=4 * 2**20),
    )(
        hidden_in, norm_gain, w_query, bias_query, w_key, w_value, bias_value, w_out, visible_end
    )


def solution(mesh):
    placed = (
        P("section", "tensor", None),
        P("section", None),
        P("section", None, "tensor"),
        P("section", "tensor"),
        P("section", "tensor", None),
        P("section", "tensor", None),
        P("section", None),
        P("section", "tensor", None),
        P("section", None),
    )
    return jax.shard_map(
        on_device,
        mesh=mesh,
        in_specs=placed,
        out_specs=P("section", "tensor", None),
        check_vma=False,
    )
```

```python
import jax
import jax.numpy as jnp
from jax import lax
from jax.experimental import pallas as pl
from jax.experimental.pallas import tpu as pltpu
from jax.sharding import PartitionSpec as P

MESH = pl.DeviceIdType.MESH
BF = jnp.bfloat16
F32 = jnp.float32
HEAD = 128
RELAYED = 4
UP_FRONT = (4, 4, 6)
KV_STEPS = (2, 5, 4)
FIRST = 2
STEPS = (2, 4, 5, 7)
LOG2E = 1.4426950408889634


def mo(value, by):
    return pl.multiple_of(value, by)


def layer(
    hidden, gain, wq, bq, wk, wv, bv, wo, ends, out,
    G, WQ, WKV, WO, ACC, KVT, KVIN, Q, KV, CTX, BQ, E, END, KID, HID, STG, RELAY,
    ag_s, ag_r, rs_s, rs_r, ho_s, ho_r, rl_s, rl_r, hid_l, wkv_l, wkv_s, wkv_r, kvt_s, kvt_r,
    wq_l, wq_s, wq_r, wo_l, wo_s, wo_r, bq_s, bq_r, kv_s, kv_r, free,
):
    section = lax.axis_index("section")
    place = lax.axis_index("tensor")
    y, h, c = lax.div(place, 4), lax.rem(lax.div(place, 2), 2), lax.rem(place, 2)
    chip = lax.div(place, 2)

    def block(dy, flip):
        return lax.rem(y + dy, 4) * 2 + (1 - h if flip else h)

    def peer(dy, flip):
        return block(dy, flip) * 2 + c

    yp, ym, xx = peer(1, 0), peer(3, 0), peer(0, 1)
    other = chip * 2 + (1 - c)
    own = chip
    nxt, prv = lax.rem(section + 1, 8), lax.rem(section + 7, 8)
    half, z = lax.div(section, 4), lax.rem(section, 4)
    first, last = z == 0, z == 3

    def send(src, dst, ss, rs, to):
        return pltpu.make_async_remote_copy(
            src_ref=src, dst_ref=dst, send_sem=ss, recv_sem=rs,
            device_id={"tensor": to}, device_id_type=MESH,
        )

    def wq_local(j):
        return pltpu.make_async_copy(
            wq.at[0, pl.ds(mo(j * 1024, 1024), 1024), :],
            WQ.at[j, :, pl.ds(mo(c * 512, 512), 512)],
            wq_l.at[j],
        )

    def wo_local(q):
        return pltpu.make_async_copy(
            wo.at[0, :, pl.ds(mo(q * 1024, 1024), 1024)],
            WO.at[q, pl.ds(mo(c * 512, 512), 512), :],
            wo_l.at[q],
        )

    def kv_local(w, n):
        return pltpu.make_async_copy(
            w.at[0], WKV.at[n, pl.ds(mo(c * 512, 512), 512), :], wkv_l.at[n]
        )

    def kv_push(w, n):
        there = WKV.at[n, pl.ds(mo(c * 512, 512), 512), :]
        return send(w.at[0], there, wkv_s.at[n], wkv_r.at[n], other)

    def wq_push(j):
        return send(
            wq.at[0, pl.ds(mo(j * 1024, 1024), 1024), :],
            WQ.at[j, :, pl.ds(mo(c * 512, 512), 512)],
            wq_s.at[j], wq_r.at[j], other,
        )

    def wo_push(q):
        return send(
            wo.at[0, :, pl.ds(mo(q * 1024, 1024), 1024)],
            WO.at[q, pl.ds(mo(c * 512, 512), 512), :],
            wo_s.at[q], wo_r.at[q], other,
        )

    def piece(b, j, lo=0, n=64):
        return G.at[j, pl.ds(mo(b * 64 + lo, 32), n), :]

    def gather(kind, j):
        b = (own, own, own, block(0, 1), block(0, 1), block(3, 0), block(1, 0), block(2, 0))[kind]
        to = (yp, ym, xx, yp, ym, yp, ym, xx)[kind]
        part = piece(b, j, 32 if kind == 6 else 0, 32 if kind in (5, 6) else 64)
        return send(part, part, ag_s.at[kind, j], ag_r.at[kind, j], to)

    def gather_side(kind):
        b = block(3, 0) if kind == 3 else block(1, 0)
        part = piece(b, b)
        return send(part, part, ag_s.at[kind, block(0, 1)], ag_r.at[kind, b], xx)

    def gathered(kind, j):
        b = (block(3, 0), block(1, 0), block(0, 1), block(3, 1), block(1, 1),
             block(2, 0), block(2, 0), block(2, 1))[kind]
        part = piece(b, j, 32 if kind == 6 else 0, 32 if kind in (5, 6) else 64)
        send(part, part, ag_s.at[kind, j], ag_r.at[kind, j], xx).wait_recv()

    def kv_sum(kind):
        b = (block(3, 0), block(1, 0), block(0, 1), block(3, 1), block(1, 1),
             block(2, 0), block(2, 0), block(2, 1))[kind]
        lo, n = (256 if kind == 6 else 0), (256 if kind in (5, 6) else 512)
        to = (ym, yp, xx, ym, yp, ym, yp, xx)[kind]
        into = (0, 1, 2, 3, 4, 5, 5, 6)[kind]
        return send(
            KVT.at[b, lo : lo + n, :], KVIN.at[into, lo : lo + n, :],
            kvt_s.at[kind], kvt_r.at[kind], to,
        )

    def kv_came(kind):
        lo, n = (256 if kind == 6 else 0), (256 if kind in (5, 6) else 512)
        into = (0, 1, 2, 3, 4, 5, 5, 6)[kind]
        part = KVIN.at[into, lo : lo + n, :]
        send(part, part, kvt_s.at[kind], kvt_r.at[kind], xx).wait_recv()
        return KVIN[into, lo : lo + n, :].astype(F32)

    order = (
        block(1, 1), block(3, 1), block(2, 1), block(2, 0), block(0, 1), block(1, 0), block(3, 0), own,
    )

    def lands(kind, k):
        line, n = (0, 64, 128, 192, 256, 320, 352, 384)[kind], 32 if kind in (5, 6) else 64
        return G.at[k, line : line + n, :]

    def reduce(kind, k):
        at, n = (384, 320, 256, 64, 0, 192, 224, 128)[kind], 32 if kind in (5, 6) else 64
        to = (ym, yp, xx, ym, yp, ym, yp, xx)[kind]
        return send(
            WQ.at[k, at : at + n, :], lands(kind, k), rs_s.at[kind, k], rs_r.at[kind, k], to
        )

    def arrived(kind, k):
        part = lands(kind, k)
        send(part, part, rs_s.at[kind, k], rs_r.at[kind, k], xx).wait_recv()
        return part[...].astype(F32)

    def term(k, at, n=64):
        return WQ[k, at : at + n, :].astype(F32)

    def hand_to(src, dst, ss, rs, to):
        return pltpu.make_async_remote_copy(
            src_ref=src, dst_ref=dst, send_sem=ss, recv_sem=rs,
            device_id={"section": to}, device_id_type=MESH,
        )

    def hand(k):
        columns = pl.ds(mo(k * 1024, 1024), 1024)
        return hand_to(STG.at[:, columns], out.at[0, :, columns], ho_s.at[k], ho_r.at[k], nxt)

    def relay_in(k):
        columns = pl.ds(mo(k * 1024, 1024), 1024)
        return hand_to(STG.at[:, columns], RELAY.at[k], ho_s.at[k], rl_r.at[k], half * 4)

    def relay_out(k):
        columns = pl.ds(mo(k * 1024, 1024), 1024)
        to = (1 - half) * 4
        return hand_to(RELAY.at[k], out.at[0, :, columns], rl_s.at[k], ho_r.at[k], to)

    hid_copy = pltpu.make_async_copy(hidden.at[0], HID, hid_l.at[0])
    hid_copy.start()
    for n, w in enumerate((wk, wv)):
        kv_local(w, n).start()
    for j in range(8):
        wq_local(j).start()
    for q in range(8):
        wo_local(q).start()

    barrier = pltpu.get_barrier_semaphore()
    for to in (yp, ym, xx, other):
        pl.semaphore_signal(barrier, inc=1, device_id={"tensor": to}, device_id_type=MESH)
    pl.semaphore_signal(barrier, inc=1, device_id={"section": prv}, device_id_type=MESH)

    @pl.when(first)
    def _():
        for to in (half * 4 + 3, (1 - half) * 4):
            pl.semaphore_signal(barrier, inc=1, device_id={"section": to}, device_id_type=MESH)

    @pl.when(first | last)
    def _():
        pl.semaphore_wait(barrier, 6)

    @pl.when(jnp.logical_not(first | last))
    def _():
        pl.semaphore_wait(barrier, 5)


    for n, w in enumerate((wk, wv)):
        kv_push(w, n).start()

    def norm_rows(rg, carry):
        rows = HID[pl.ds(mo(rg * 16, 16), 16), :].astype(F32)
        power = jnp.mean(rows * rows, axis=-1, keepdims=True)
        scale = lax.rsqrt(power + 1e-06)
        normed = (rows * scale * gain[...].astype(F32)).astype(BF)
        for j in range(8):
            G[j, pl.ds(mo(own * 64 + rg * 16, 16), 16), :] = normed[:, j * 1024 : (j + 1) * 1024]
        return carry

    hid_copy.wait()
    lax.fori_loop(0, 4, norm_rows, 0)
    rest = [block(0, 0), block(0, 1), block(1, 1), block(3, 1)]
    own_order = (
        [block(1, 0), block(2, 0), block(2, 1), block(3, 0), *rest],
        [block(3, 0), block(2, 0), block(2, 1), block(1, 0), *rest],
        [block(0, 1), block(1, 1), block(3, 1), block(2, 1), block(0, 0), block(1, 0), block(2, 0), block(3, 0)],
    )
    for n in range(8):
        for kind in range(3):
            if n < UP_FRONT[kind]:
                gather(kind, own_order[kind][n]).start()
    BQ[c] = jnp.broadcast_to(bq[...], (16, 512))
    bias_push = send(BQ.at[c], BQ.at[c], bq_s.at[0], bq_r.at[0], other)
    bias_push.start()
    for j in range(8):
        wq_push(j).start()
    for q in range(8):
        wo_push(q).start()
    ACC[...] = jnp.zeros_like(ACC)
    for b in range(8):
        line = jnp.broadcast_to(ends[:, b * 128 : (b + 1) * 128].astype(F32), (128, 128))
        E[b] = line.T
    lane = lax.broadcasted_iota(jnp.int32, (8, 512), 1)
    token = lane + lax.div(lane, 64) * 64
    KID[:, 0:512] = token.astype(F32)
    KID[:, 512:1024] = (token + 64).astype(F32)
    KV[:, 256:384] = jnp.ones((1024, 128), BF)
    for n, b in enumerate(order):
        END[n * 64 : (n + 1) * 64, :] = E[b, pl.ds(mo(c * 64, 64), 64), :]

    def project(first, last, j):
        rows = slice(first * 64, last * 64)
        normed = jnp.concatenate(
            [G[j, pl.ds(mo(b * 64, 64), 64), :] for b in order[first:last]], axis=0
        )
        for n in range(2):
            columns = slice(n * 512, (n + 1) * 512)
            ACC[rows, columns] += jnp.dot(normed, WQ[j, :, columns], preferred_element_type=F32)

    def queries(first, last):
        rows = slice(first * 64, last * 64)
        for n in range(2):
            columns = slice(n * 512, (n + 1) * 512)
            Q[rows, columns] = (ACC[rows, columns] + BQ[n, 0:1, :].astype(F32)).astype(BF)

    gathered(0, block(1, 0))
    gather(5, block(1, 0)).start()
    gathered(1, block(3, 0))
    gather(6, block(3, 0)).start()
    gathered(2, block(1, 0))
    gather(3, block(1, 0)).start()
    gathered(2, block(3, 0))
    gather(4, block(3, 0)).start()
    gathered(0, block(1, 1))
    gather(5, block(1, 1)).start()
    gathered(1, block(3, 1))
    gather(6, block(3, 1)).start()
    for n in range(8):
        for kind in range(2):
            if n >= UP_FRONT[kind]:
                gather(kind, own_order[kind][n]).start()
    gathered(5, block(0, 1))
    gathered(6, block(0, 1))
    gather(7, block(0, 1)).start()
    for n in range(UP_FRONT[2], 8):
        gather(2, own_order[2][n]).start()
    gathered(0, own)
    gather(5, own).start()
    gathered(1, own)
    gather(6, own).start()
    for kind in range(2, 8):
        gathered(kind, own)

    for n, w in enumerate((wk, wv)):
        kv_local(w, n).wait()
        part = WKV.at[n, pl.ds(mo((1 - c) * 512, 512), 512), :]
        send(part, part, wkv_s.at[n], wkv_r.at[n], other).wait_recv()
        for m in range(2):
            sums = jnp.dot(
                G[own], WKV[n, :, m * 512 : (m + 1) * 512], preferred_element_type=F32
            ).astype(BF)
            for b in range(4):
                KVT[m * 4 + b, :, n * HEAD : (n + 1) * HEAD] = sums[:, b * HEAD : (b + 1) * HEAD]
    for kind in (7, 3, 4):
        kv_sum(kind).start()

    def pass_along(j, carry):
        @pl.when((j != block(1, 0)) & (j != block(1, 1)) & (j != own))
        def _():
            gathered(0, j)
            gather(5, j).start()

        @pl.when((j != block(3, 0)) & (j != block(3, 1)) & (j != own))
        def _():
            gathered(1, j)
            gather(6, j).start()

        return carry

    lax.fori_loop(0, 8, pass_along, 0)
    gather_side(3).start()
    gather_side(4).start()

    def pass_across(j, carry):
        @pl.when((j != block(1, 0)) & (j != block(3, 0)) & (j != own))
        def _():
            gathered(2, j)

        @pl.when((j != block(1, 0)) & (j != block(0, 1)))
        def _():
            gather(3, j).start()

        @pl.when((j != block(3, 0)) & (j != block(0, 1)))
        def _():
            gather(4, j).start()

        @pl.when(j != block(0, 1))
        def _():
            @pl.when(j != own)
            def _():
                gathered(5, j)
                gathered(6, j)

            gather(7, j).start()

        @pl.when(j == KV_STEPS[0])
        def _():
            b = block(2, 0)
            KVT[b] = (KVT[b].astype(F32) + kv_came(7)).astype(BF)
            kv_sum(5).start()
            kv_sum(6).start()
            b = block(0, 1)
            KVT[b] = (KVT[b].astype(F32) + kv_came(3) + kv_came(4)).astype(BF)
            kv_sum(2).start()

        @pl.when(j == KV_STEPS[1])
        def _():
            b = block(3, 0)
            KVT[b, 0:256, :] = (KVT[b, 0:256, :].astype(F32) + kv_came(5)).astype(BF)
            kv_sum(0).start()
            b = block(1, 0)
            KVT[b, 256:512, :] = (KVT[b, 256:512, :].astype(F32) + kv_came(6)).astype(BF)
            kv_sum(1).start()

        wq_local(j).wait()
        part = WQ.at[j, :, pl.ds(mo((1 - c) * 512, 512), 512)]
        send(part, part, wq_s.at[j], wq_r.at[j], other).wait_recv()
        project(4, 8, j)
        return carry

    lax.fori_loop(0, 8, pass_across, 0)

    def project_far(j, carry):
        @pl.when(j != own)
        def _():
            gathered(7, j)

        project(2, 4, j)

        @pl.when(j != own)
        def _():
            gathered(3, j)
            gathered(4, j)

        project(0, 2, j)

        @pl.when(j == KV_STEPS[2])
        def _():
            total = KVT[own].astype(F32) + kv_came(0) + kv_came(1) + kv_came(2)
            rows = pl.ds(mo(c * 512, 512), 512)
            KV[rows, 0:HEAD] = total[:, 0:HEAD].astype(BF)
            bias = bv[:, pl.ds(mo(chip * HEAD, HEAD), HEAD)].astype(F32)
            KV[rows, HEAD : 2 * HEAD] = (total[:, HEAD:] + bias).astype(BF)
            part = KV.at[rows, 0 : 2 * HEAD]
            send(part, part, kv_s.at[0], kv_r.at[0], other).start()

        return carry

    lax.fori_loop(0, 8, project_far, 0)

    def gather_sent(j, carry):
        for kind in range(8):
            gather(kind, j).wait_send()
        return carry

    lax.fori_loop(0, 8, gather_sent, 0)
    for to in (yp, ym, xx):
        pl.semaphore_signal(free, inc=1, device_id={"tensor": to}, device_id_type=MESH)
    send(BQ.at[1 - c], BQ.at[1 - c], bq_s.at[0], bq_r.at[0], other).wait_recv()
    queries(0, 2)
    part = KV.at[pl.ds(mo((1 - c) * 512, 512), 512), 0 : 2 * HEAD]
    send(part, part, kv_s.at[0], kv_r.at[0], other).wait_recv()

    def attend(first, last, head, heads):
        rows = slice(first * 64, last * 64)
        columns = [pl.ds(mo((head + n) * HEAD, HEAD), HEAD) for n in range(heads)]
        query = jnp.concatenate([Q[rows, at] for at in columns], axis=0)
        end = jnp.concatenate([END[rows, 0:1]] * heads, axis=0)
        scores = lax.dot_general(
            query, KV[:, 0:HEAD], (((1,), (1,)), ((), ())), preferred_element_type=F32
        )
        scores = jnp.where(KID[0:1, :] < end, scores, -1e30 * HEAD**0.5)
        top = jnp.max(scores, axis=-1, keepdims=True)
        expo = jnp.exp2((scores - top) * (LOG2E / HEAD**0.5)).astype(BF)
        mixed = jnp.dot(expo, KV[:, HEAD : 3 * HEAD], preferred_element_type=F32)
        mixed = (mixed[:, :HEAD] / mixed[:, HEAD:]).astype(BF)
        count = (last - first) * 64
        for n, at in enumerate(columns):
            CTX[rows, at] = mixed[n * count : (n + 1) * count]

    def terms(first, last, k):
        rows = slice(first * 64, last * 64)
        WQ[k, rows, :] = jnp.dot(CTX[rows, :], WO[k], preferred_element_type=F32).astype(BF)

    def attend_two(first):
        def pair_of(pair, carry):
            attend(first, first + 2, pair * 2, 2)
            return carry

        lax.fori_loop(0, 4, pair_of, 0)

    def side(k):
        wo_local(k).wait()
        part = WO.at[k, pl.ds(mo((1 - c) * 512, 512), 512), :]
        send(part, part, wo_s.at[k], wo_r.at[k], other).wait_recv()
        terms(0, 2, k)
        reduce(3, k).start()
        reduce(4, k).start()

    attend_two(0)
    pl.semaphore_wait(free, 3)
    for k in range(FIRST):
        side(k)
    queries(2, 8)
    attend_two(2)

    def step(i, carry):
        @pl.when(i < 8)
        def _():
            terms(2, 4, i)
            reduce(7, i).start()

        @pl.when(i < 8 - FIRST)
        def _():
            side(i + FIRST)

        @pl.when(i < 4)
        def _():
            attend(4, 8, 2 * i, 1)
            attend(4, 8, 2 * i + 1, 1)

        def at(steps, work):
            @pl.when((i >= steps) & (i < 8 + steps))
            def _():
                work(i - steps)

        at(STEPS[0], opposite)
        at(STEPS[1], across)
        at(STEPS[2], near)
        at(STEPS[3], finish)
        return carry

    def opposite(k):
        WQ[k, 192:256, :] = (term(k, 192) + arrived(7, k)).astype(BF)
        reduce(5, k).start()
        reduce(6, k).start()

    def across(k):
        terms(4, 8, k)
        WQ[k, 256:320, :] = (term(k, 256) + arrived(3, k) + arrived(4, k)).astype(BF)
        reduce(2, k).start()

    def near(k):
        WQ[k, 384:416, :] = (term(k, 384, 32) + arrived(5, k)).astype(BF)
        reduce(0, k).start()
        WQ[k, 352:384, :] = (term(k, 352, 32) + arrived(6, k)).astype(BF)
        reduce(1, k).start()

    def finish(k):
        columns = pl.ds(mo(k * 1024, 1024), 1024)
        total = term(k, 448) + arrived(0, k) + arrived(1, k) + arrived(2, k)
        STG[:, columns] = (HID[:, columns].astype(F32) + total).astype(BF)

        @pl.when(last & (k < RELAYED))
        def _():
            relay_in(k).start()

        @pl.when(jnp.logical_not(last & (k < RELAYED)))
        def _():
            hand(k).start()

        @pl.when(first & (k >= 2) & (k < 2 + RELAYED))
        def _():
            relay_in(k - 2).wait_recv()
            relay_out(k - 2).start()

    lax.fori_loop(0, 8 + STEPS[3], step, 0)

    def sent(k, carry):
        for kind in range(8):
            reduce(kind, k).wait_send()
        hand(k).wait()

        @pl.when(first & (k < RELAYED))
        def _():
            relay_out(k).wait_send()

        return carry

    lax.fori_loop(0, 8, sent, 0)
    for n, w in enumerate((wk, wv)):
        kv_push(w, n).wait_send()
    for kind in range(8):
        kv_sum(kind).wait_send()
    for j in range(8):
        wq_push(j).wait_send()
    for q in range(8):
        wo_push(q).wait_send()
    bias_push.wait_send()
    part = KV.at[pl.ds(mo(c * 512, 512), 512), 0 : 2 * HEAD]
    send(part, part, kv_s.at[0], kv_r.at[0], other).wait_send()


def on_device(
    hidden_in, norm_gain, w_query, bias_query, w_key, w_value, bias_value, w_out, visible_end
):
    vmem, anywhere = pl.BlockSpec(memory_space=pltpu.VMEM), pl.BlockSpec(memory_space=pl.ANY)
    dma = pltpu.SemaphoreType.DMA
    return pl.pallas_call(
        layer,
        out_shape=jax.ShapeDtypeStruct(hidden_in.shape, BF),
        in_specs=[anywhere, vmem, anywhere, vmem, anywhere, anywhere, vmem, anywhere, vmem],
        out_specs=anywhere,
        scratch_shapes=[
            pltpu.VMEM((8, 512, 1024), BF),
            pltpu.VMEM((8, 1024, 1024), BF),
            pltpu.VMEM((2, 1024, 1024), BF),
            pltpu.VMEM((8, 1024, 1024), BF),
            pltpu.VMEM((512, 1024), F32),
            pltpu.VMEM((8, 512, 256), BF),
            pltpu.VMEM((7, 512, 256), BF),
            pltpu.VMEM((512, 1024), BF),
            pltpu.VMEM((1024, 384), BF),
            pltpu.VMEM((512, 1024), BF),
            pltpu.VMEM((2, 16, 512), BF),
            pltpu.VMEM((8, 128, 128), F32),
            pltpu.VMEM((512, 128), F32),
            pltpu.VMEM((8, 1024), F32),
            pltpu.VMEM((64, 8192), BF),
            pltpu.VMEM((64, 8192), BF),
            pltpu.VMEM((RELAYED, 64, 1024), BF),
            dma((8, 8)), dma((8, 8)), dma((8, 8)), dma((8, 8)), dma((8,)), dma((8,)), dma((8,)), dma((8,)),
            dma((1,)), dma((2,)), dma((2,)), dma((2,)), dma((8,)), dma((8,)),
            dma((8,)), dma((8,)), dma((8,)), dma((8,)), dma((8,)), dma((8,)),
            dma((1,)), dma((1,)), dma((1,)), dma((1,)), pltpu.SemaphoreType.REGULAR,
        ],
        compiler_params=pltpu.CompilerParams(
            collective_id=0, has_side_effects=True, vmem_limit_bytes=63 * 2**20
        ),
        cost_estimate=pl.CostEstimate(flops=24 * 10**9, bytes_accessed=40 * 10**6, transcendentals=4 * 2**20),
    )(
        hidden_in, norm_gain, w_query, bias_query, w_key, w_value, bias_value, w_out, visible_end
    )


def solution(mesh):
    placed = (
        P("section", "tensor", None),
        P("section", None),
        P("section", None, "tensor"),
        P("section", "tensor"),
        P("section", "tensor", None),
        P("section", "tensor", None),
        P("section", None),
        P("section", "tensor", None),
        P("section", None),
    )
    return jax.shard_map(
        on_device,
        mesh=mesh,
        in_specs=placed,
        out_specs=P("section", "tensor", None),
        check_vma=False,
    )
```

```python
import jax
import jax.numpy as jnp
from jax import lax
from jax.experimental import pallas as pl
from jax.experimental.pallas import tpu as pltpu
from jax.sharding import PartitionSpec as P

MESH = pl.DeviceIdType.MESH
BF = jnp.bfloat16
F32 = jnp.float32
HEAD = 128
RELAYED = 4
UP_FRONT = (4, 4, 6)
KV_STEPS = (2, 5, 4)
FIRST = 2
STEPS = (2, 4, 5, 7)
STACK = 4
LOG2E = 1.4426950408889634


def mo(value, by):
    return pl.multiple_of(value, by)


def layer(
    hidden, gain, wq, bq, wk, wv, bv, wo, ends, out,
    G, WQ, WKV, WO, ACC, KVT, KVIN, Q, KV, CTX, BQ, E, END, KID, HID, STG, RELAY,
    ag_s, ag_r, rs_s, rs_r, ho_s, ho_r, rl_s, rl_r, hid_l, wkv_l, wkv_s, wkv_r, kvt_s, kvt_r,
    wq_l, wq_s, wq_r, wo_l, wo_s, wo_r, bq_s, bq_r, kv_s, kv_r, free,
):
    section = lax.axis_index("section")
    place = lax.axis_index("tensor")
    y, h, c = lax.div(place, 4), lax.rem(lax.div(place, 2), 2), lax.rem(place, 2)
    chip = lax.div(place, 2)

    def block(dy, flip):
        return lax.rem(y + dy, 4) * 2 + (1 - h if flip else h)

    def peer(dy, flip):
        return block(dy, flip) * 2 + c

    yp, ym, xx = peer(1, 0), peer(3, 0), peer(0, 1)
    other = chip * 2 + (1 - c)
    own = chip
    nxt, prv = lax.rem(section + 1, 8), lax.rem(section + 7, 8)
    half, z = lax.div(section, 4), lax.rem(section, 4)
    first, last = z == 0, z == 3

    def send(src, dst, ss, rs, to):
        return pltpu.make_async_remote_copy(
            src_ref=src, dst_ref=dst, send_sem=ss, recv_sem=rs,
            device_id={"tensor": to}, device_id_type=MESH,
        )

    def wq_local(j):
        return pltpu.make_async_copy(
            wq.at[0, pl.ds(mo(j * 1024, 1024), 1024), :],
            WQ.at[j, :, pl.ds(mo(c * 512, 512), 512)],
            wq_l.at[j],
        )

    def wo_local(q):
        return pltpu.make_async_copy(
            wo.at[0, :, pl.ds(mo(q * 1024, 1024), 1024)],
            WO.at[q, pl.ds(mo(c * 512, 512), 512), :],
            wo_l.at[q],
        )

    def kv_local(w, n):
        return pltpu.make_async_copy(
            w.at[0], WKV.at[n, pl.ds(mo(c * 512, 512), 512), :], wkv_l.at[n]
        )

    def kv_push(w, n):
        there = WKV.at[n, pl.ds(mo(c * 512, 512), 512), :]
        return send(w.at[0], there, wkv_s.at[n], wkv_r.at[n], other)

    def wq_push(j):
        return send(
            wq.at[0, pl.ds(mo(j * 1024, 1024), 1024), :],
            WQ.at[j, :, pl.ds(mo(c * 512, 512), 512)],
            wq_s.at[j], wq_r.at[j], other,
        )

    def wo_push(q):
        return send(
            wo.at[0, :, pl.ds(mo(q * 1024, 1024), 1024)],
            WO.at[q, pl.ds(mo(c * 512, 512), 512), :],
            wo_s.at[q], wo_r.at[q], other,
        )

    def piece(b, j, lo=0, n=64):
        return G.at[j, pl.ds(mo(b * 64 + lo, 32), n), :]

    def gather(kind, j):
        b = (own, own, own, block(0, 1), block(0, 1), block(3, 0), block(1, 0), block(2, 0))[kind]
        to = (yp, ym, xx, yp, ym, yp, ym, xx)[kind]
        part = piece(b, j, 32 if kind == 6 else 0, 32 if kind in (5, 6) else 64)
        return send(part, part, ag_s.at[kind, j], ag_r.at[kind, j], to)

    def gather_side(kind):
        b = block(3, 0) if kind == 3 else block(1, 0)
        part = piece(b, b)
        return send(part, part, ag_s.at[kind, block(0, 1)], ag_r.at[kind, b], xx)

    def gathered(kind, j):
        b = (block(3, 0), block(1, 0), block(0, 1), block(3, 1), block(1, 1),
             block(2, 0), block(2, 0), block(2, 1))[kind]
        part = piece(b, j, 32 if kind == 6 else 0, 32 if kind in (5, 6) else 64)
        send(part, part, ag_s.at[kind, j], ag_r.at[kind, j], xx).wait_recv()

    def kv_sum(kind):
        b = (block(3, 0), block(1, 0), block(0, 1), block(3, 1), block(1, 1),
             block(2, 0), block(2, 0), block(2, 1))[kind]
        lo, n = (256 if kind == 6 else 0), (256 if kind in (5, 6) else 512)
        to = (ym, yp, xx, ym, yp, ym, yp, xx)[kind]
        into = (0, 1, 2, 3, 4, 5, 5, 6)[kind]
        return send(
            KVT.at[b, lo : lo + n, :], KVIN.at[into, lo : lo + n, :],
            kvt_s.at[kind], kvt_r.at[kind], to,
        )

    def kv_came(kind):
        lo, n = (256 if kind == 6 else 0), (256 if kind in (5, 6) else 512)
        into = (0, 1, 2, 3, 4, 5, 5, 6)[kind]
        part = KVIN.at[into, lo : lo + n, :]
        send(part, part, kvt_s.at[kind], kvt_r.at[kind], xx).wait_recv()
        return KVIN[into, lo : lo + n, :].astype(F32)

    order = (
        block(1, 1), block(3, 1), block(2, 1), block(2, 0), block(0, 1), block(1, 0), block(3, 0), own,
    )

    def lands(kind, k):
        line, n = (0, 64, 128, 192, 256, 320, 352, 384)[kind], 32 if kind in (5, 6) else 64
        return G.at[k, line : line + n, :]

    def reduce(kind, k):
        at, n = (384, 320, 256, 64, 0, 192, 224, 128)[kind], 32 if kind in (5, 6) else 64
        to = (ym, yp, xx, ym, yp, ym, yp, xx)[kind]
        return send(
            WQ.at[k, at : at + n, :], lands(kind, k), rs_s.at[kind, k], rs_r.at[kind, k], to
        )

    def arrived(kind, k):
        part = lands(kind, k)
        send(part, part, rs_s.at[kind, k], rs_r.at[kind, k], xx).wait_recv()
        return part[...].astype(F32)

    def term(k, at, n=64):
        return WQ[k, at : at + n, :].astype(F32)

    def hand_to(src, dst, ss, rs, to):
        return pltpu.make_async_remote_copy(
            src_ref=src, dst_ref=dst, send_sem=ss, recv_sem=rs,
            device_id={"section": to}, device_id_type=MESH,
        )

    def hand(k):
        columns = pl.ds(mo(k * 1024, 1024), 1024)
        return hand_to(STG.at[:, columns], out.at[0, :, columns], ho_s.at[k], ho_r.at[k], nxt)

    def relay_in(k):
        columns = pl.ds(mo(k * 1024, 1024), 1024)
        return hand_to(STG.at[:, columns], RELAY.at[k], ho_s.at[k], rl_r.at[k], half * 4)

    def relay_out(k):
        columns = pl.ds(mo(k * 1024, 1024), 1024)
        to = (1 - half) * 4
        return hand_to(RELAY.at[k], out.at[0, :, columns], rl_s.at[k], ho_r.at[k], to)

    hid_copy = pltpu.make_async_copy(hidden.at[0], HID, hid_l.at[0])
    hid_copy.start()
    barrier = pltpu.get_barrier_semaphore()
    for to in (yp, ym, xx, other):
        pl.semaphore_signal(barrier, inc=1, device_id={"tensor": to}, device_id_type=MESH)
    pl.semaphore_signal(barrier, inc=1, device_id={"section": prv}, device_id_type=MESH)

    @pl.when(first)
    def _():
        for to in (half * 4 + 3, (1 - half) * 4):
            pl.semaphore_signal(barrier, inc=1, device_id={"section": to}, device_id_type=MESH)

    for n, w in enumerate((wk, wv)):
        kv_local(w, n).start()
    for j in range(8):
        wq_local(j).start()
    for q in range(8):
        wo_local(q).start()

    def norm_rows(rg, carry):
        rows = HID[pl.ds(mo(rg * 16, 16), 16), :].astype(F32)
        power = jnp.mean(rows * rows, axis=-1, keepdims=True)
        scale = lax.rsqrt(power + 1e-06)
        normed = (rows * scale * gain[...].astype(F32)).astype(BF)
        for j in range(8):
            G[j, pl.ds(mo(own * 64 + rg * 16, 16), 16), :] = normed[:, j * 1024 : (j + 1) * 1024]
        return carry

    hid_copy.wait()
    lax.fori_loop(0, 4, norm_rows, 0)

    @pl.when(first | last)
    def _():
        pl.semaphore_wait(barrier, 6)

    @pl.when(jnp.logical_not(first | last))
    def _():
        pl.semaphore_wait(barrier, 5)


    for n, w in enumerate((wk, wv)):
        kv_push(w, n).start()

    rest = [block(0, 0), block(0, 1), block(1, 1), block(3, 1)]
    own_order = (
        [block(1, 0), block(2, 0), block(2, 1), block(3, 0), *rest],
        [block(3, 0), block(2, 0), block(2, 1), block(1, 0), *rest],
        [block(0, 1), block(1, 1), block(3, 1), block(2, 1), block(0, 0), block(1, 0), block(2, 0), block(3, 0)],
    )
    for n in range(8):
        for kind in range(3):
            if n < UP_FRONT[kind]:
                gather(kind, own_order[kind][n]).start()
    BQ[c] = jnp.broadcast_to(bq[...], (16, 512))
    bias_push = send(BQ.at[c], BQ.at[c], bq_s.at[0], bq_r.at[0], other)
    bias_push.start()
    for j in range(8):
        wq_push(j).start()
    for q in range(8):
        wo_push(q).start()
    ACC[...] = jnp.zeros_like(ACC)
    for b in range(8):
        line = jnp.broadcast_to(ends[:, b * 128 : (b + 1) * 128].astype(F32), (128, 128))
        E[b] = line.T
    lane = lax.broadcasted_iota(jnp.int32, (8, 512), 1)
    token = lane + lax.div(lane, 64) * 64
    KID[:, 0:512] = token.astype(F32)
    KID[:, 512:1024] = (token + 64).astype(F32)
    KV[:, 256:384] = jnp.ones((1024, 128), BF)
    for n, b in enumerate(order):
        END[n * 64 : (n + 1) * 64, :] = E[b, pl.ds(mo(c * 64, 64), 64), :]

    def project(first, last, j):
        rows = slice(first * 64, last * 64)
        normed = jnp.concatenate(
            [G[j, pl.ds(mo(b * 64, 64), 64), :] for b in order[first:last]], axis=0
        )
        for n in range(2):
            columns = slice(n * 512, (n + 1) * 512)
            ACC[rows, columns] += jnp.dot(normed, WQ[j, :, columns], preferred_element_type=F32)

    def queries(first, last):
        rows = slice(first * 64, last * 64)
        for n in range(2):
            columns = slice(n * 512, (n + 1) * 512)
            Q[rows, columns] = (ACC[rows, columns] + BQ[n, 0:1, :].astype(F32)).astype(BF)

    gathered(0, block(1, 0))
    gather(5, block(1, 0)).start()
    gathered(1, block(3, 0))
    gather(6, block(3, 0)).start()
    gathered(2, block(1, 0))
    gather(3, block(1, 0)).start()
    gathered(2, block(3, 0))
    gather(4, block(3, 0)).start()
    gathered(0, block(1, 1))
    gather(5, block(1, 1)).start()
    gathered(1, block(3, 1))
    gather(6, block(3, 1)).start()
    for n in range(8):
        for kind in range(2):
            if n >= UP_FRONT[kind]:
                gather(kind, own_order[kind][n]).start()
    gathered(5, block(0, 1))
    gathered(6, block(0, 1))
    gather(7, block(0, 1)).start()
    for n in range(UP_FRONT[2], 8):
        gather(2, own_order[2][n]).start()
    gathered(0, own)
    gather(5, own).start()
    gathered(1, own)
    gather(6, own).start()
    for kind in range(2, 8):
        gathered(kind, own)

    for n, w in enumerate((wk, wv)):
        kv_local(w, n).wait()
        part = WKV.at[n, pl.ds(mo((1 - c) * 512, 512), 512), :]
        send(part, part, wkv_s.at[n], wkv_r.at[n], other).wait_recv()
        for m in range(2):
            sums = jnp.dot(
                G[own], WKV[n, :, m * 512 : (m + 1) * 512], preferred_element_type=F32
            ).astype(BF)
            for b in range(4):
                KVT[m * 4 + b, :, n * HEAD : (n + 1) * HEAD] = sums[:, b * HEAD : (b + 1) * HEAD]
    for kind in (7, 3, 4):
        kv_sum(kind).start()

    def pass_along(j, carry):
        @pl.when((j != block(1, 0)) & (j != block(1, 1)) & (j != own))
        def _():
            gathered(0, j)
            gather(5, j).start()

        @pl.when((j != block(3, 0)) & (j != block(3, 1)) & (j != own))
        def _():
            gathered(1, j)
            gather(6, j).start()

        return carry

    lax.fori_loop(0, 8, pass_along, 0)
    gather_side(3).start()
    gather_side(4).start()

    def pass_across(j, carry):
        @pl.when((j != block(1, 0)) & (j != block(3, 0)) & (j != own))
        def _():
            gathered(2, j)

        @pl.when((j != block(1, 0)) & (j != block(0, 1)))
        def _():
            gather(3, j).start()

        @pl.when((j != block(3, 0)) & (j != block(0, 1)))
        def _():
            gather(4, j).start()

        @pl.when(j != block(0, 1))
        def _():
            @pl.when(j != own)
            def _():
                gathered(5, j)
                gathered(6, j)

            gather(7, j).start()

        @pl.when(j == KV_STEPS[0])
        def _():
            b = block(2, 0)
            KVT[b] = (KVT[b].astype(F32) + kv_came(7)).astype(BF)
            kv_sum(5).start()
            kv_sum(6).start()
            b = block(0, 1)
            KVT[b] = (KVT[b].astype(F32) + kv_came(3) + kv_came(4)).astype(BF)
            kv_sum(2).start()

        @pl.when(j == KV_STEPS[1])
        def _():
            b = block(3, 0)
            KVT[b, 0:256, :] = (KVT[b, 0:256, :].astype(F32) + kv_came(5)).astype(BF)
            kv_sum(0).start()
            b = block(1, 0)
            KVT[b, 256:512, :] = (KVT[b, 256:512, :].astype(F32) + kv_came(6)).astype(BF)
            kv_sum(1).start()

        wq_local(j).wait()
        part = WQ.at[j, :, pl.ds(mo((1 - c) * 512, 512), 512)]
        send(part, part, wq_s.at[j], wq_r.at[j], other).wait_recv()
        project(4, 8, j)
        return carry

    lax.fori_loop(0, 8, pass_across, 0)

    def project_far(j, carry):
        @pl.when(j != own)
        def _():
            gathered(7, j)

        project(2, 4, j)

        @pl.when(j != own)
        def _():
            gathered(3, j)
            gathered(4, j)

        project(0, 2, j)
        for kind in range(8):
            gather(kind, j).wait_send()

        @pl.when(j == KV_STEPS[2])
        def _():
            total = KVT[own].astype(F32) + kv_came(0) + kv_came(1) + kv_came(2)
            rows = pl.ds(mo(c * 512, 512), 512)
            KV[rows, 0:HEAD] = total[:, 0:HEAD].astype(BF)
            bias = bv[:, pl.ds(mo(chip * HEAD, HEAD), HEAD)].astype(F32)
            KV[rows, HEAD : 2 * HEAD] = (total[:, HEAD:] + bias).astype(BF)
            part = KV.at[rows, 0 : 2 * HEAD]
            send(part, part, kv_s.at[0], kv_r.at[0], other).start()

        return carry

    lax.fori_loop(0, 8, project_far, 0)

    for to in (yp, ym, xx):
        pl.semaphore_signal(free, inc=1, device_id={"tensor": to}, device_id_type=MESH)
    send(BQ.at[1 - c], BQ.at[1 - c], bq_s.at[0], bq_r.at[0], other).wait_recv()
    queries(0, 2)
    part = KV.at[pl.ds(mo((1 - c) * 512, 512), 512), 0 : 2 * HEAD]
    send(part, part, kv_s.at[0], kv_r.at[0], other).wait_recv()

    def attend(first, last, head, heads):
        rows = slice(first * 64, last * 64)
        columns = [pl.ds(mo((head + n) * HEAD, HEAD), HEAD) for n in range(heads)]
        query = jnp.concatenate([Q[rows, at] for at in columns], axis=0)
        end = jnp.concatenate([END[rows, 0:1]] * heads, axis=0)
        scores = lax.dot_general(
            query, KV[:, 0:HEAD], (((1,), (1,)), ((), ())), preferred_element_type=F32
        )
        scores = jnp.where(KID[0:1, :] < end, scores, -1e30 * HEAD**0.5)
        top = jnp.max(scores, axis=-1, keepdims=True)
        expo = jnp.exp2((scores - top) * (LOG2E / HEAD**0.5)).astype(BF)
        mixed = jnp.dot(expo, KV[:, HEAD : 3 * HEAD], preferred_element_type=F32)
        mixed = (mixed[:, :HEAD] / mixed[:, HEAD:]).astype(BF)
        count = (last - first) * 64
        for n, at in enumerate(columns):
            CTX[rows, at] = mixed[n * count : (n + 1) * count]

    def terms(first, last, k):
        rows = slice(first * 64, last * 64)
        WQ[k, rows, :] = jnp.dot(CTX[rows, :], WO[k], preferred_element_type=F32).astype(BF)

    def attend_two(first):
        def group(n, carry):
            attend(first, first + 2, n * STACK, STACK)
            return carry

        lax.fori_loop(0, 8 // STACK, group, 0)

    def side(k):
        wo_local(k).wait()
        part = WO.at[k, pl.ds(mo((1 - c) * 512, 512), 512), :]
        send(part, part, wo_s.at[k], wo_r.at[k], other).wait_recv()
        terms(0, 2, k)
        reduce(3, k).start()
        reduce(4, k).start()

    attend_two(0)
    pl.semaphore_wait(free, 3)
    for k in range(FIRST):
        side(k)
    queries(2, 8)
    attend_two(2)

    def step(i, carry):
        @pl.when(i < 8)
        def _():
            terms(2, 4, i)
            reduce(7, i).start()

        @pl.when(i < 8 - FIRST)
        def _():
            side(i + FIRST)

        @pl.when(i < 4)
        def _():
            attend(4, 8, 2 * i, 2)

        def at(steps, work):
            @pl.when((i >= steps) & (i < 8 + steps))
            def _():
                work(i - steps)

        at(STEPS[0], opposite)
        at(STEPS[1], across)
        at(STEPS[2], near)
        at(STEPS[3], finish)
        return carry

    def opposite(k):
        WQ[k, 192:256, :] = (term(k, 192) + arrived(7, k)).astype(BF)
        reduce(5, k).start()
        reduce(6, k).start()

    def across(k):
        terms(4, 8, k)
        WQ[k, 256:320, :] = (term(k, 256) + arrived(3, k) + arrived(4, k)).astype(BF)
        reduce(2, k).start()

    def near(k):
        WQ[k, 384:416, :] = (term(k, 384, 32) + arrived(5, k)).astype(BF)
        reduce(0, k).start()
        WQ[k, 352:384, :] = (term(k, 352, 32) + arrived(6, k)).astype(BF)
        reduce(1, k).start()

    def finish(k):
        columns = pl.ds(mo(k * 1024, 1024), 1024)
        total = term(k, 448) + arrived(0, k) + arrived(1, k) + arrived(2, k)
        STG[:, columns] = (HID[:, columns].astype(F32) + total).astype(BF)

        @pl.when(last & (k < RELAYED))
        def _():
            relay_in(k).start()

        @pl.when(jnp.logical_not(last & (k < RELAYED)))
        def _():
            hand(k).start()

        @pl.when(first & (k >= 2) & (k < 2 + RELAYED))
        def _():
            relay_in(k - 2).wait_recv()
            relay_out(k - 2).start()

    lax.fori_loop(0, 8 + STEPS[3], step, 0)

    def sent(k, carry):
        for kind in range(8):
            reduce(kind, k).wait_send()
        hand(k).wait_send()

        @pl.when(first & (k < RELAYED))
        def _():
            relay_out(k).wait_send()

        return carry

    lax.fori_loop(0, 8, sent, 0)
    for n, w in enumerate((wk, wv)):
        kv_push(w, n).wait_send()
    for kind in range(8):
        kv_sum(kind).wait_send()
    for j in range(8):
        wq_push(j).wait_send()
    for q in range(8):
        wo_push(q).wait_send()
    bias_push.wait_send()
    part = KV.at[pl.ds(mo(c * 512, 512), 512), 0 : 2 * HEAD]
    send(part, part, kv_s.at[0], kv_r.at[0], other).wait_send()


    def handed(k, carry):
        hand(k).wait_recv()
        return carry

    lax.fori_loop(0, 8, handed, 0)


def on_device(
    hidden_in, norm_gain, w_query, bias_query, w_key, w_value, bias_value, w_out, visible_end
):
    vmem, anywhere = pl.BlockSpec(memory_space=pltpu.VMEM), pl.BlockSpec(memory_space=pl.ANY)
    dma = pltpu.SemaphoreType.DMA
    return pl.pallas_call(
        layer,
        out_shape=jax.ShapeDtypeStruct(hidden_in.shape, BF),
        in_specs=[anywhere, vmem, anywhere, vmem, anywhere, anywhere, vmem, anywhere, vmem],
        out_specs=anywhere,
        scratch_shapes=[
            pltpu.VMEM((8, 512, 1024), BF),
            pltpu.VMEM((8, 1024, 1024), BF),
            pltpu.VMEM((2, 1024, 1024), BF),
            pltpu.VMEM((8, 1024, 1024), BF),
            pltpu.VMEM((512, 1024), F32),
            pltpu.VMEM((8, 512, 256), BF),
            pltpu.VMEM((7, 512, 256), BF),
            pltpu.VMEM((512, 1024), BF),
            pltpu.VMEM((1024, 384), BF),
            pltpu.VMEM((512, 1024), BF),
            pltpu.VMEM((2, 16, 512), BF),
            pltpu.VMEM((8, 128, 128), F32),
            pltpu.VMEM((512, 128), F32),
            pltpu.VMEM((8, 1024), F32),
            pltpu.VMEM((64, 8192), BF),
            pltpu.VMEM((64, 8192), BF),
            pltpu.VMEM((RELAYED, 64, 1024), BF),
            dma((8, 8)), dma((8, 8)), dma((8, 8)), dma((8, 8)), dma((8,)), dma((8,)), dma((8,)), dma((8,)),
            dma((1,)), dma((2,)), dma((2,)), dma((2,)), dma((8,)), dma((8,)),
            dma((8,)), dma((8,)), dma((8,)), dma((8,)), dma((8,)), dma((8,)),
            dma((1,)), dma((1,)), dma((1,)), dma((1,)), pltpu.SemaphoreType.REGULAR,
        ],
        compiler_params=pltpu.CompilerParams(
            collective_id=0, has_side_effects=True, vmem_limit_bytes=63 * 2**20
        ),
        cost_estimate=pl.CostEstimate(flops=24 * 10**9, bytes_accessed=40 * 10**6, transcendentals=4 * 2**20),
    )(
        hidden_in, norm_gain, w_query, bias_query, w_key, w_value, bias_value, w_out, visible_end
    )


def solution(mesh):
    placed = (
        P("section", "tensor", None),
        P("section", None),
        P("section", None, "tensor"),
        P("section", "tensor"),
        P("section", "tensor", None),
        P("section", "tensor", None),
        P("section", None),
        P("section", "tensor", None),
        P("section", None),
    )
    return jax.shard_map(
        on_device,
        mesh=mesh,
        in_specs=placed,
        out_specs=P("section", "tensor", None),
        check_vma=False,
    )
```

```python
import jax
import jax.numpy as jnp
from jax import lax
from jax.experimental import pallas as pl
from jax.experimental.pallas import tpu as pltpu
from jax.sharding import PartitionSpec as P

MESH = pl.DeviceIdType.MESH
BF = jnp.bfloat16
F32 = jnp.float32
HEAD = 128
RELAYED = 4
UP_FRONT = (4, 4, 6)
KV_STEPS = (2, 5, 4)
FIRST = 2
STEPS = (2, 4, 5, 7)
STACK = 4
LOG2E = 1.4426950408889634


def mo(value, by):
    return pl.multiple_of(value, by)


def layer(
    hidden, gain, wq, bq, wk, wv, bv, wo, ends, out,
    G, WQ, WKV, WO, ACC, KVT, KVIN, Q, KV, CTX, BQ, E, END, KID, HID, STG, RELAY,
    ag_s, ag_r, rs_s, rs_r, ho_s, ho_r, rl_s, rl_r, hs_s, hs_r, hid_l, wkv_l, wkv_s, wkv_r, kvt_s, kvt_r,
    wq_l, wq_s, wq_r, wo_l, wo_s, wo_r, bq_s, bq_r, kv_s, kv_r, free,
):
    section = lax.axis_index("section")
    place = lax.axis_index("tensor")
    y, h, c = lax.div(place, 4), lax.rem(lax.div(place, 2), 2), lax.rem(place, 2)
    chip = lax.div(place, 2)

    def block(dy, flip):
        return lax.rem(y + dy, 4) * 2 + (1 - h if flip else h)

    def peer(dy, flip):
        return block(dy, flip) * 2 + c

    yp, ym, xx = peer(1, 0), peer(3, 0), peer(0, 1)
    other = chip * 2 + (1 - c)
    own = chip
    nxt, prv = lax.rem(section + 1, 8), lax.rem(section + 7, 8)
    half, z = lax.div(section, 4), lax.rem(section, 4)
    first, last = z == 0, z == 3

    def send(src, dst, ss, rs, to):
        return pltpu.make_async_remote_copy(
            src_ref=src, dst_ref=dst, send_sem=ss, recv_sem=rs,
            device_id={"tensor": to}, device_id_type=MESH,
        )

    def wq_local(j):
        return pltpu.make_async_copy(
            wq.at[0, pl.ds(mo(j * 1024, 1024), 1024), :],
            WQ.at[j, :, pl.ds(mo(c * 512, 512), 512)],
            wq_l.at[j],
        )

    def wo_local(q):
        return pltpu.make_async_copy(
            wo.at[0, :, pl.ds(mo(q * 1024, 1024), 1024)],
            WO.at[q, pl.ds(mo(c * 512, 512), 512), :],
            wo_l.at[q],
        )

    def kv_local(w, n):
        return pltpu.make_async_copy(
            w.at[0], WKV.at[n, pl.ds(mo(c * 512, 512), 512), :], wkv_l.at[n]
        )

    def kv_push(w, n):
        there = WKV.at[n, pl.ds(mo(c * 512, 512), 512), :]
        return send(w.at[0], there, wkv_s.at[n], wkv_r.at[n], other)

    def wq_push(j):
        return send(
            wq.at[0, pl.ds(mo(j * 1024, 1024), 1024), :],
            WQ.at[j, :, pl.ds(mo(c * 512, 512), 512)],
            wq_s.at[j], wq_r.at[j], other,
        )

    def wo_push(q):
        return send(
            wo.at[0, :, pl.ds(mo(q * 1024, 1024), 1024)],
            WO.at[q, pl.ds(mo(c * 512, 512), 512), :],
            wo_s.at[q], wo_r.at[q], other,
        )

    def piece(b, j, lo=0, n=64):
        return G.at[j, pl.ds(mo(b * 64 + lo, 32), n), :]

    def gather(kind, j):
        b = (own, own, own, block(0, 1), block(0, 1), block(3, 0), block(1, 0), block(2, 0))[kind]
        to = (yp, ym, xx, yp, ym, yp, ym, xx)[kind]
        part = piece(b, j, 32 if kind == 6 else 0, 32 if kind in (5, 6) else 64)
        return send(part, part, ag_s.at[kind, j], ag_r.at[kind, j], to)

    def gather_side(kind):
        b = block(3, 0) if kind == 3 else block(1, 0)
        part = piece(b, b)
        return send(part, part, ag_s.at[kind, block(0, 1)], ag_r.at[kind, b], xx)

    def gather_half(kind):
        j = block(2, 1)
        part = piece(block(0, 1), j, 0, 32)
        return send(part, part, ag_s.at[kind, j], ag_r.at[kind, j], yp if kind == 3 else ym)

    def gather_half_side(kind):
        b, j = (block(3, 0), block(1, 0)) if kind == 3 else (block(1, 0), block(3, 0))
        part = piece(b, j, 32, 32)
        return send(part, part, hs_s.at[kind - 3], hs_r.at[kind - 3], xx)

    def gathered_side(kind, j):
        b, halved = (block(3, 1), block(1, 1)) if kind == 3 else (block(1, 1), block(3, 1))

        @pl.when(j != halved)
        def _():
            gathered(kind, j)

        @pl.when(j == halved)
        def _():
            part = piece(b, j, 0, 32)
            send(part, part, ag_s.at[kind, j], ag_r.at[kind, j], xx).wait_recv()
            part = piece(b, j, 32, 32)
            send(part, part, hs_s.at[kind - 3], hs_r.at[kind - 3], xx).wait_recv()

    def gathered(kind, j):
        b = (block(3, 0), block(1, 0), block(0, 1), block(3, 1), block(1, 1),
             block(2, 0), block(2, 0), block(2, 1))[kind]
        part = piece(b, j, 32 if kind == 6 else 0, 32 if kind in (5, 6) else 64)
        send(part, part, ag_s.at[kind, j], ag_r.at[kind, j], xx).wait_recv()

    def kv_sum(kind):
        b = (block(3, 0), block(1, 0), block(0, 1), block(3, 1), block(1, 1),
             block(2, 0), block(2, 0), block(2, 1))[kind]
        lo, n = (256 if kind == 6 else 0), (256 if kind in (5, 6) else 512)
        to = (ym, yp, xx, ym, yp, ym, yp, xx)[kind]
        into = (0, 1, 2, 3, 4, 5, 5, 6)[kind]
        return send(
            KVT.at[b, lo : lo + n, :], KVIN.at[into, lo : lo + n, :],
            kvt_s.at[kind], kvt_r.at[kind], to,
        )

    def kv_came(kind):
        lo, n = (256 if kind == 6 else 0), (256 if kind in (5, 6) else 512)
        into = (0, 1, 2, 3, 4, 5, 5, 6)[kind]
        part = KVIN.at[into, lo : lo + n, :]
        send(part, part, kvt_s.at[kind], kvt_r.at[kind], xx).wait_recv()
        return KVIN[into, lo : lo + n, :].astype(F32)

    order = (
        block(1, 1), block(3, 1), block(2, 1), block(2, 0), block(0, 1), block(1, 0), block(3, 0), own,
    )

    def lands(kind, k):
        line, n = (0, 64, 128, 192, 256, 320, 352, 384)[kind], 32 if kind in (5, 6) else 64
        return G.at[k, line : line + n, :]

    def reduce(kind, k):
        at, n = (384, 320, 256, 64, 0, 192, 224, 128)[kind], 32 if kind in (5, 6) else 64
        to = (ym, yp, xx, ym, yp, ym, yp, xx)[kind]
        return send(
            WQ.at[k, at : at + n, :], lands(kind, k), rs_s.at[kind, k], rs_r.at[kind, k], to
        )

    def arrived(kind, k):
        part = lands(kind, k)
        send(part, part, rs_s.at[kind, k], rs_r.at[kind, k], xx).wait_recv()
        return part[...].astype(F32)

    def term(k, at, n=64):
        return WQ[k, at : at + n, :].astype(F32)

    def hand_to(src, dst, ss, rs, to):
        return pltpu.make_async_remote_copy(
            src_ref=src, dst_ref=dst, send_sem=ss, recv_sem=rs,
            device_id={"section": to}, device_id_type=MESH,
        )

    def hand(k):
        columns = pl.ds(mo(k * 1024, 1024), 1024)
        return hand_to(STG.at[:, columns], out.at[0, :, columns], ho_s.at[k], ho_r.at[k], nxt)

    def relay_in(k):
        columns = pl.ds(mo(k * 1024, 1024), 1024)
        return hand_to(STG.at[:, columns], RELAY.at[k], ho_s.at[k], rl_r.at[k], half * 4)

    def relay_out(k):
        columns = pl.ds(mo(k * 1024, 1024), 1024)
        to = (1 - half) * 4
        return hand_to(RELAY.at[k], out.at[0, :, columns], rl_s.at[k], ho_r.at[k], to)

    hid_copy = pltpu.make_async_copy(hidden.at[0], HID, hid_l.at[0])
    hid_copy.start()
    barrier = pltpu.get_barrier_semaphore()
    for to in (yp, ym, xx, other):
        pl.semaphore_signal(barrier, inc=1, device_id={"tensor": to}, device_id_type=MESH)
    pl.semaphore_signal(barrier, inc=1, device_id={"section": prv}, device_id_type=MESH)

    @pl.when(first)
    def _():
        for to in (half * 4 + 3, (1 - half) * 4):
            pl.semaphore_signal(barrier, inc=1, device_id={"section": to}, device_id_type=MESH)

    for n, w in enumerate((wk, wv)):
        kv_local(w, n).start()
    for j in range(8):
        wq_local(j).start()
    for q in range(8):
        wo_local(q).start()

    def norm_rows(rg, carry):
        rows = HID[pl.ds(mo(rg * 16, 16), 16), :].astype(F32)
        power = jnp.mean(rows * rows, axis=-1, keepdims=True)
        scale = lax.rsqrt(power + 1e-06)
        normed = (rows * scale * gain[...].astype(F32)).astype(BF)
        for j in range(8):
            G[j, pl.ds(mo(own * 64 + rg * 16, 16), 16), :] = normed[:, j * 1024 : (j + 1) * 1024]
        return carry

    hid_copy.wait()
    lax.fori_loop(0, 4, norm_rows, 0)

    @pl.when(first | last)
    def _():
        pl.semaphore_wait(barrier, 6)

    @pl.when(jnp.logical_not(first | last))
    def _():
        pl.semaphore_wait(barrier, 5)


    for n, w in enumerate((wk, wv)):
        kv_push(w, n).start()

    rest = [block(0, 0), block(0, 1), block(1, 1), block(3, 1)]
    own_order = (
        [block(1, 0), block(2, 0), block(2, 1), block(3, 0), *rest],
        [block(3, 0), block(2, 0), block(2, 1), block(1, 0), *rest],
        [block(0, 1), block(1, 1), block(3, 1), block(2, 1), block(0, 0), block(1, 0), block(2, 0), block(3, 0)],
    )
    for n in range(8):
        for kind in range(3):
            if n < UP_FRONT[kind]:
                gather(kind, own_order[kind][n]).start()
    BQ[c] = jnp.broadcast_to(bq[...], (16, 512))
    bias_push = send(BQ.at[c], BQ.at[c], bq_s.at[0], bq_r.at[0], other)
    bias_push.start()
    for j in range(8):
        wq_push(j).start()
    for q in range(8):
        wo_push(q).start()
    ACC[...] = jnp.zeros_like(ACC)
    for b in range(8):
        line = jnp.broadcast_to(ends[:, b * 128 : (b + 1) * 128].astype(F32), (128, 128))
        E[b] = line.T
    lane = lax.broadcasted_iota(jnp.int32, (8, 512), 1)
    token = lane + lax.div(lane, 64) * 64
    KID[:, 0:512] = token.astype(F32)
    KID[:, 512:1024] = (token + 64).astype(F32)
    KV[:, 256:384] = jnp.ones((1024, 128), BF)
    for n, b in enumerate(order):
        END[n * 64 : (n + 1) * 64, :] = E[b, pl.ds(mo(c * 64, 64), 64), :]

    def project(first, last, j):
        rows = slice(first * 64, last * 64)
        normed = jnp.concatenate(
            [G[j, pl.ds(mo(b * 64, 64), 64), :] for b in order[first:last]], axis=0
        )
        for n in range(2):
            columns = slice(n * 512, (n + 1) * 512)
            ACC[rows, columns] += jnp.dot(normed, WQ[j, :, columns], preferred_element_type=F32)

    def queries(first, last):
        rows = slice(first * 64, last * 64)
        for n in range(2):
            columns = slice(n * 512, (n + 1) * 512)
            Q[rows, columns] = (ACC[rows, columns] + BQ[n, 0:1, :].astype(F32)).astype(BF)

    gathered(0, block(1, 0))
    gather(5, block(1, 0)).start()
    gathered(1, block(3, 0))
    gather(6, block(3, 0)).start()
    gathered(2, block(1, 0))
    gather(3, block(1, 0)).start()
    gathered(2, block(3, 0))
    gather(4, block(3, 0)).start()
    gathered(0, block(1, 1))
    gather(5, block(1, 1)).start()
    gathered(1, block(3, 1))
    gather(6, block(3, 1)).start()
    for n in range(8):
        for kind in range(2):
            if n >= UP_FRONT[kind]:
                gather(kind, own_order[kind][n]).start()
    gathered(5, block(0, 1))
    gathered(6, block(0, 1))
    gather(7, block(0, 1)).start()
    for n in range(UP_FRONT[2], 8):
        gather(2, own_order[2][n]).start()
    gathered(0, own)
    gather(5, own).start()
    gathered(1, own)
    gather(6, own).start()
    for kind in range(2, 8):
        gathered(kind, own)

    for n, w in enumerate((wk, wv)):
        kv_local(w, n).wait()
        part = WKV.at[n, pl.ds(mo((1 - c) * 512, 512), 512), :]
        send(part, part, wkv_s.at[n], wkv_r.at[n], other).wait_recv()
        for m in range(2):
            sums = jnp.dot(
                G[own], WKV[n, :, m * 512 : (m + 1) * 512], preferred_element_type=F32
            ).astype(BF)
            for b in range(4):
                KVT[m * 4 + b, :, n * HEAD : (n + 1) * HEAD] = sums[:, b * HEAD : (b + 1) * HEAD]
    for kind in (7, 3, 4):
        kv_sum(kind).start()

    def pass_along(j, carry):
        @pl.when((j != block(1, 0)) & (j != block(1, 1)) & (j != own))
        def _():
            gathered(0, j)
            gather(5, j).start()

        @pl.when((j != block(3, 0)) & (j != block(3, 1)) & (j != own))
        def _():
            gathered(1, j)
            gather(6, j).start()

        return carry

    lax.fori_loop(0, 8, pass_along, 0)
    gather_side(3).start()
    gather_side(4).start()
    gather_half_side(3).start()
    gather_half_side(4).start()

    def pass_across(j, carry):
        @pl.when((j != block(1, 0)) & (j != block(3, 0)) & (j != own))
        def _():
            gathered(2, j)

        @pl.when((j != block(1, 0)) & (j != block(0, 1)) & (j != block(2, 1)))
        def _():
            gather(3, j).start()

        @pl.when((j != block(3, 0)) & (j != block(0, 1)) & (j != block(2, 1)))
        def _():
            gather(4, j).start()

        @pl.when(j == block(2, 1))
        def _():
            gather_half(3).start()
            gather_half(4).start()

        @pl.when(j != block(0, 1))
        def _():
            @pl.when(j != own)
            def _():
                gathered(5, j)
                gathered(6, j)

            gather(7, j).start()

        @pl.when(j == KV_STEPS[0])
        def _():
            b = block(2, 0)
            KVT[b] = (KVT[b].astype(F32) + kv_came(7)).astype(BF)
            kv_sum(5).start()
            kv_sum(6).start()
            b = block(0, 1)
            KVT[b] = (KVT[b].astype(F32) + kv_came(3) + kv_came(4)).astype(BF)
            kv_sum(2).start()

        @pl.when(j == KV_STEPS[1])
        def _():
            b = block(3, 0)
            KVT[b, 0:256, :] = (KVT[b, 0:256, :].astype(F32) + kv_came(5)).astype(BF)
            kv_sum(0).start()
            b = block(1, 0)
            KVT[b, 256:512, :] = (KVT[b, 256:512, :].astype(F32) + kv_came(6)).astype(BF)
            kv_sum(1).start()

        wq_local(j).wait()
        part = WQ.at[j, :, pl.ds(mo((1 - c) * 512, 512), 512)]
        send(part, part, wq_s.at[j], wq_r.at[j], other).wait_recv()
        project(4, 8, j)
        return carry

    lax.fori_loop(0, 8, pass_across, 0)

    def project_far(j, carry):
        @pl.when(j != own)
        def _():
            gathered(7, j)

        project(2, 4, j)

        @pl.when(j != own)
        def _():
            gathered_side(3, j)
            gathered_side(4, j)

        project(0, 2, j)
        for kind in (0, 1, 2, 5, 6, 7):
            gather(kind, j).wait_send()

        @pl.when(j != block(2, 1))
        def _():
            gather(3, j).wait_send()
            gather(4, j).wait_send()

        @pl.when(j == block(2, 1))
        def _():
            for kind in (3, 4):
                gather_half(kind).wait_send()
                gather_half_side(kind).wait_send()

        @pl.when(j == KV_STEPS[2])
        def _():
            total = KVT[own].astype(F32) + kv_came(0) + kv_came(1) + kv_came(2)
            rows = pl.ds(mo(c * 512, 512), 512)
            KV[rows, 0:HEAD] = total[:, 0:HEAD].astype(BF)
            bias = bv[:, pl.ds(mo(chip * HEAD, HEAD), HEAD)].astype(F32)
            KV[rows, HEAD : 2 * HEAD] = (total[:, HEAD:] + bias).astype(BF)
            part = KV.at[rows, 0 : 2 * HEAD]
            send(part, part, kv_s.at[0], kv_r.at[0], other).start()

        return carry

    lax.fori_loop(0, 8, project_far, 0)

    for to in (yp, ym, xx):
        pl.semaphore_signal(free, inc=1, device_id={"tensor": to}, device_id_type=MESH)
    send(BQ.at[1 - c], BQ.at[1 - c], bq_s.at[0], bq_r.at[0], other).wait_recv()
    queries(0, 2)
    part = KV.at[pl.ds(mo((1 - c) * 512, 512), 512), 0 : 2 * HEAD]
    send(part, part, kv_s.at[0], kv_r.at[0], other).wait_recv()

    def attend(first, last, head, heads):
        rows = slice(first * 64, last * 64)
        columns = [pl.ds(mo((head + n) * HEAD, HEAD), HEAD) for n in range(heads)]
        query = jnp.concatenate([Q[rows, at] for at in columns], axis=0)
        end = jnp.concatenate([END[rows, 0:1]] * heads, axis=0)
        scores = lax.dot_general(
            query, KV[:, 0:HEAD], (((1,), (1,)), ((), ())), preferred_element_type=F32
        )
        scores = jnp.where(KID[0:1, :] < end, scores, -1e30 * HEAD**0.5)
        top = jnp.max(scores, axis=-1, keepdims=True)
        expo = jnp.exp2((scores - top) * (LOG2E / HEAD**0.5)).astype(BF)
        mixed = jnp.dot(expo, KV[:, HEAD : 3 * HEAD], preferred_element_type=F32)
        mixed = (mixed[:, :HEAD] / mixed[:, HEAD:]).astype(BF)
        count = (last - first) * 64
        for n, at in enumerate(columns):
            CTX[rows, at] = mixed[n * count : (n + 1) * count]

    def terms(first, last, k):
        rows = slice(first * 64, last * 64)
        WQ[k, rows, :] = jnp.dot(CTX[rows, :], WO[k], preferred_element_type=F32).astype(BF)

    def attend_two(first):
        def group(n, carry):
            attend(first, first + 2, n * STACK, STACK)
            return carry

        lax.fori_loop(0, 8 // STACK, group, 0)

    def side(k):
        wo_local(k).wait()
        part = WO.at[k, pl.ds(mo((1 - c) * 512, 512), 512), :]
        send(part, part, wo_s.at[k], wo_r.at[k], other).wait_recv()
        terms(0, 2, k)
        reduce(3, k).start()
        reduce(4, k).start()

    attend_two(0)
    pl.semaphore_wait(free, 3)
    for k in range(FIRST):
        side(k)
    queries(2, 8)
    attend_two(2)

    def step(i, carry):
        @pl.when(i < 8)
        def _():
            terms(2, 4, i)
            reduce(7, i).start()

        @pl.when(i < 8 - FIRST)
        def _():
            side(i + FIRST)

        @pl.when(i < 4)
        def _():
            attend(4, 8, 2 * i, 2)

        def at(steps, work):
            @pl.when((i >= steps) & (i < 8 + steps))
            def _():
                work(i - steps)

        at(STEPS[0], opposite)
        at(STEPS[1], across)
        at(STEPS[2], near)
        at(STEPS[3], finish)
        return carry

    def opposite(k):
        WQ[k, 192:256, :] = (term(k, 192) + arrived(7, k)).astype(BF)
        reduce(5, k).start()
        reduce(6, k).start()

    def across(k):
        terms(4, 8, k)
        WQ[k, 256:320, :] = (term(k, 256) + arrived(3, k) + arrived(4, k)).astype(BF)
        reduce(2, k).start()

    def near(k):
        WQ[k, 384:416, :] = (term(k, 384, 32) + arrived(5, k)).astype(BF)
        reduce(0, k).start()
        WQ[k, 352:384, :] = (term(k, 352, 32) + arrived(6, k)).astype(BF)
        reduce(1, k).start()

    def finish(k):
        columns = pl.ds(mo(k * 1024, 1024), 1024)
        total = term(k, 448) + arrived(0, k) + arrived(1, k) + arrived(2, k)
        STG[:, columns] = (HID[:, columns].astype(F32) + total).astype(BF)

        @pl.when(last & (k < RELAYED))
        def _():
            relay_in(k).start()

        @pl.when(jnp.logical_not(last & (k < RELAYED)))
        def _():
            hand(k).start()

        @pl.when(first & (k >= 2) & (k < 2 + RELAYED))
        def _():
            relay_in(k - 2).wait_recv()
            relay_out(k - 2).start()

    lax.fori_loop(0, 8 + STEPS[3], step, 0)

    def sent(k, carry):
        for kind in range(8):
            reduce(kind, k).wait_send()
        hand(k).wait_send()

        @pl.when(first & (k < RELAYED))
        def _():
            relay_out(k).wait_send()

        return carry

    lax.fori_loop(0, 8, sent, 0)
    for n, w in enumerate((wk, wv)):
        kv_push(w, n).wait_send()
    for kind in range(8):
        kv_sum(kind).wait_send()
    for j in range(8):
        wq_push(j).wait_send()
    for q in range(8):
        wo_push(q).wait_send()
    bias_push.wait_send()
    part = KV.at[pl.ds(mo(c * 512, 512), 512), 0 : 2 * HEAD]
    send(part, part, kv_s.at[0], kv_r.at[0], other).wait_send()


    def handed(k, carry):
        hand(k).wait_recv()
        return carry

    lax.fori_loop(0, 8, handed, 0)


def on_device(
    hidden_in, norm_gain, w_query, bias_query, w_key, w_value, bias_value, w_out, visible_end
):
    vmem, anywhere = pl.BlockSpec(memory_space=pltpu.VMEM), pl.BlockSpec(memory_space=pl.ANY)
    dma = pltpu.SemaphoreType.DMA
    return pl.pallas_call(
        layer,
        out_shape=jax.ShapeDtypeStruct(hidden_in.shape, BF),
        in_specs=[anywhere, vmem, anywhere, vmem, anywhere, anywhere, vmem, anywhere, vmem],
        out_specs=anywhere,
        scratch_shapes=[
            pltpu.VMEM((8, 512, 1024), BF),
            pltpu.VMEM((8, 1024, 1024), BF),
            pltpu.VMEM((2, 1024, 1024), BF),
            pltpu.VMEM((8, 1024, 1024), BF),
            pltpu.VMEM((512, 1024), F32),
            pltpu.VMEM((8, 512, 256), BF),
            pltpu.VMEM((7, 512, 256), BF),
            pltpu.VMEM((512, 1024), BF),
            pltpu.VMEM((1024, 384), BF),
            pltpu.VMEM((512, 1024), BF),
            pltpu.VMEM((2, 16, 512), BF),
            pltpu.VMEM((8, 128, 128), F32),
            pltpu.VMEM((512, 128), F32),
            pltpu.VMEM((8, 1024), F32),
            pltpu.VMEM((64, 8192), BF),
            pltpu.VMEM((64, 8192), BF),
            pltpu.VMEM((RELAYED, 64, 1024), BF),
            dma((8, 8)), dma((8, 8)), dma((8, 8)), dma((8, 8)), dma((8,)), dma((8,)), dma((8,)), dma((8,)),
            dma((2,)), dma((2,)),
            dma((1,)), dma((2,)), dma((2,)), dma((2,)), dma((8,)), dma((8,)),
            dma((8,)), dma((8,)), dma((8,)), dma((8,)), dma((8,)), dma((8,)),
            dma((1,)), dma((1,)), dma((1,)), dma((1,)), pltpu.SemaphoreType.REGULAR,
        ],
        compiler_params=pltpu.CompilerParams(
            collective_id=0, has_side_effects=True, vmem_limit_bytes=63 * 2**20
        ),
        cost_estimate=pl.CostEstimate(flops=24 * 10**9, bytes_accessed=40 * 10**6, transcendentals=4 * 2**20),
    )(
        hidden_in, norm_gain, w_query, bias_query, w_key, w_value, bias_value, w_out, visible_end
    )


def solution(mesh):
    placed = (
        P("section", "tensor", None),
        P("section", None),
        P("section", None, "tensor"),
        P("section", "tensor"),
        P("section", "tensor", None),
        P("section", "tensor", None),
        P("section", None),
        P("section", "tensor", None),
        P("section", None),
    )
    return jax.shard_map(
        on_device,
        mesh=mesh,
        in_specs=placed,
        out_specs=P("section", "tensor", None),
        check_vma=False,
    )
```

```python
import jax
import jax.numpy as jnp
from jax import lax
from jax.experimental import pallas as pl
from jax.experimental.pallas import tpu as pltpu
from jax.sharding import PartitionSpec as P

MESH = pl.DeviceIdType.MESH
BF = jnp.bfloat16
F32 = jnp.float32
HEAD = 128
RELAYED = 4
UP_FRONT = (4, 4, 6)
KV_STEPS = (2, 5, 4)
FIRST = 1
STEPS = (2, 4, 5, 7)
STACK = 4
LOG2E = 1.4426950408889634


def mo(value, by):
    return pl.multiple_of(value, by)


def layer(
    hidden, gain, wq, bq, wk, wv, bv, wo, ends, out,
    G, WQ, WKV, WO, ACC, KVT, KVIN, Q, KV, CTX, BQ, E, END, KID, HID, STG, RELAY,
    ag_s, ag_r, rs_s, rs_r, ho_s, ho_r, rl_s, rl_r, hs_s, hs_r, hid_l, wkv_l, wkv_s, wkv_r, kvt_s, kvt_r,
    wq_l, wq_s, wq_r, wo_l, wo_s, wo_r, bq_s, bq_r, kv_s, kv_r, free,
):
    section = lax.axis_index("section")
    place = lax.axis_index("tensor")
    y, h, c = lax.div(place, 4), lax.rem(lax.div(place, 2), 2), lax.rem(place, 2)
    chip = lax.div(place, 2)

    def block(dy, flip):
        return lax.rem(y + dy, 4) * 2 + (1 - h if flip else h)

    def peer(dy, flip):
        return block(dy, flip) * 2 + c

    yp, ym, xx = peer(1, 0), peer(3, 0), peer(0, 1)
    other = chip * 2 + (1 - c)
    own = chip
    nxt, prv = lax.rem(section + 1, 8), lax.rem(section + 7, 8)
    half, z = lax.div(section, 4), lax.rem(section, 4)
    first, last = z == 0, z == 3

    def send(src, dst, ss, rs, to):
        return pltpu.make_async_remote_copy(
            src_ref=src, dst_ref=dst, send_sem=ss, recv_sem=rs,
            device_id={"tensor": to}, device_id_type=MESH,
        )

    def wq_local(j):
        return pltpu.make_async_copy(
            wq.at[0, pl.ds(mo(j * 1024, 1024), 1024), :],
            WQ.at[j, :, pl.ds(mo(c * 512, 512), 512)],
            wq_l.at[j],
        )

    def wo_local(q):
        return pltpu.make_async_copy(
            wo.at[0, :, pl.ds(mo(q * 1024, 1024), 1024)],
            WO.at[q, pl.ds(mo(c * 512, 512), 512), :],
            wo_l.at[q],
        )

    def kv_local(w, n):
        return pltpu.make_async_copy(
            w.at[0], WKV.at[n, pl.ds(mo(c * 512, 512), 512), :], wkv_l.at[n]
        )

    def kv_push(w, n):
        there = WKV.at[n, pl.ds(mo(c * 512, 512), 512), :]
        return send(w.at[0], there, wkv_s.at[n], wkv_r.at[n], other)

    def wq_push(j):
        return send(
            wq.at[0, pl.ds(mo(j * 1024, 1024), 1024), :],
            WQ.at[j, :, pl.ds(mo(c * 512, 512), 512)],
            wq_s.at[j], wq_r.at[j], other,
        )

    def wo_push(q):
        return send(
            wo.at[0, :, pl.ds(mo(q * 1024, 1024), 1024)],
            WO.at[q, pl.ds(mo(c * 512, 512), 512), :],
            wo_s.at[q], wo_r.at[q], other,
        )

    def piece(b, j, lo=0, n=64):
        return G.at[j, pl.ds(mo(b * 64 + lo, 32), n), :]

    def gather(kind, j):
        b = (own, own, own, block(0, 1), block(0, 1), block(3, 0), block(1, 0), block(2, 0))[kind]
        to = (yp, ym, xx, yp, ym, yp, ym, xx)[kind]
        part = piece(b, j, 32 if kind == 6 else 0, 32 if kind in (5, 6) else 64)
        return send(part, part, ag_s.at[kind, j], ag_r.at[kind, j], to)

    def gather_side(kind):
        b = block(3, 0) if kind == 3 else block(1, 0)
        part = piece(b, b)
        return send(part, part, ag_s.at[kind, block(0, 1)], ag_r.at[kind, b], xx)

    def gather_half(kind):
        j = block(2, 1)
        part = piece(block(0, 1), j, 0, 32)
        return send(part, part, ag_s.at[kind, j], ag_r.at[kind, j], yp if kind == 3 else ym)

    def gather_half_side(kind):
        b, j = (block(3, 0), block(1, 0)) if kind == 3 else (block(1, 0), block(3, 0))
        part = piece(b, j, 32, 32)
        return send(part, part, hs_s.at[kind - 3], hs_r.at[kind - 3], xx)

    def gathered_side(kind, j):
        b, halved = (block(3, 1), block(1, 1)) if kind == 3 else (block(1, 1), block(3, 1))

        @pl.when(j != halved)
        def _():
            gathered(kind, j)

        @pl.when(j == halved)
        def _():
            part = piece(b, j, 0, 32)
            send(part, part, ag_s.at[kind, j], ag_r.at[kind, j], xx).wait_recv()
            part = piece(b, j, 32, 32)
            send(part, part, hs_s.at[kind - 3], hs_r.at[kind - 3], xx).wait_recv()

    def gathered(kind, j):
        b = (block(3, 0), block(1, 0), block(0, 1), block(3, 1), block(1, 1),
             block(2, 0), block(2, 0), block(2, 1))[kind]
        part = piece(b, j, 32 if kind == 6 else 0, 32 if kind in (5, 6) else 64)
        send(part, part, ag_s.at[kind, j], ag_r.at[kind, j], xx).wait_recv()

    def kv_sum(kind):
        b = (block(3, 0), block(1, 0), block(0, 1), block(3, 1), block(1, 1),
             block(2, 0), block(2, 0), block(2, 1))[kind]
        lo, n = (256 if kind == 6 else 0), (256 if kind in (5, 6) else 512)
        to = (ym, yp, xx, ym, yp, ym, yp, xx)[kind]
        into = (0, 1, 2, 3, 4, 5, 5, 6)[kind]
        return send(
            KVT.at[b, lo : lo + n, :], KVIN.at[into, lo : lo + n, :],
            kvt_s.at[kind], kvt_r.at[kind], to,
        )

    def kv_came(kind):
        lo, n = (256 if kind == 6 else 0), (256 if kind in (5, 6) else 512)
        into = (0, 1, 2, 3, 4, 5, 5, 6)[kind]
        part = KVIN.at[into, lo : lo + n, :]
        send(part, part, kvt_s.at[kind], kvt_r.at[kind], xx).wait_recv()
        return KVIN[into, lo : lo + n, :].astype(F32)

    order = (
        block(1, 1), block(3, 1), block(2, 1), block(2, 0), block(0, 1), block(1, 0), block(3, 0), own,
    )

    def lands(kind, k):
        line, n = (0, 64, 128, 192, 256, 320, 352, 384)[kind], 32 if kind in (5, 6) else 64
        return G.at[k, line : line + n, :]

    def reduce(kind, k):
        at, n = (384, 320, 256, 64, 0, 192, 224, 128)[kind], 32 if kind in (5, 6) else 64
        to = (ym, yp, xx, ym, yp, ym, yp, xx)[kind]
        return send(
            WQ.at[k, at : at + n, :], lands(kind, k), rs_s.at[kind, k], rs_r.at[kind, k], to
        )

    def arrived(kind, k):
        part = lands(kind, k)
        send(part, part, rs_s.at[kind, k], rs_r.at[kind, k], xx).wait_recv()
        return part[...].astype(F32)

    def term(k, at, n=64):
        return WQ[k, at : at + n, :].astype(F32)

    def hand_to(src, dst, ss, rs, to):
        return pltpu.make_async_remote_copy(
            src_ref=src, dst_ref=dst, send_sem=ss, recv_sem=rs,
            device_id={"section": to}, device_id_type=MESH,
        )

    def hand(k):
        columns = pl.ds(mo(k * 1024, 1024), 1024)
        return hand_to(STG.at[:, columns], out.at[0, :, columns], ho_s.at[k], ho_r.at[k], nxt)

    def relay_in(k):
        columns = pl.ds(mo(k * 1024, 1024), 1024)
        return hand_to(STG.at[:, columns], RELAY.at[k], ho_s.at[k], rl_r.at[k], half * 4)

    def relay_out(k):
        columns = pl.ds(mo(k * 1024, 1024), 1024)
        to = (1 - half) * 4
        return hand_to(RELAY.at[k], out.at[0, :, columns], rl_s.at[k], ho_r.at[k], to)

    hid_copy = pltpu.make_async_copy(hidden.at[0], HID, hid_l.at[0])
    hid_copy.start()
    barrier = pltpu.get_barrier_semaphore()
    for to in (yp, ym, xx, other):
        pl.semaphore_signal(barrier, inc=1, device_id={"tensor": to}, device_id_type=MESH)
    pl.semaphore_signal(barrier, inc=1, device_id={"section": prv}, device_id_type=MESH)

    @pl.when(first)
    def _():
        for to in (half * 4 + 3, (1 - half) * 4):
            pl.semaphore_signal(barrier, inc=1, device_id={"section": to}, device_id_type=MESH)

    for n, w in enumerate((wk, wv)):
        kv_local(w, n).start()
    for j in range(8):
        wq_local(j).start()
    for q in range(8):
        wo_local(q).start()

    def norm_rows(rg, carry):
        rows = HID[pl.ds(mo(rg * 16, 16), 16), :].astype(F32)
        power = jnp.mean(rows * rows, axis=-1, keepdims=True)
        scale = lax.rsqrt(power + 1e-06)
        normed = (rows * scale * gain[...].astype(F32)).astype(BF)
        for j in range(8):
            G[j, pl.ds(mo(own * 64 + rg * 16, 16), 16), :] = normed[:, j * 1024 : (j + 1) * 1024]
        return carry

    hid_copy.wait()
    lax.fori_loop(0, 4, norm_rows, 0)

    @pl.when(first | last)
    def _():
        pl.semaphore_wait(barrier, 6)

    @pl.when(jnp.logical_not(first | last))
    def _():
        pl.semaphore_wait(barrier, 5)


    rest = [block(0, 0), block(0, 1), block(1, 1), block(3, 1)]
    own_order = (
        [block(1, 0), block(2, 0), block(2, 1), block(3, 0), *rest],
        [block(3, 0), block(2, 0), block(2, 1), block(1, 0), *rest],
        [block(0, 1), block(1, 1), block(3, 1), block(2, 1), block(0, 0), block(1, 0), block(2, 0), block(3, 0)],
    )
    for n in range(8):
        for kind in range(3):
            if n < UP_FRONT[kind]:
                gather(kind, own_order[kind][n]).start()
    for n, w in enumerate((wk, wv)):
        kv_push(w, n).start()
    BQ[c] = jnp.broadcast_to(bq[...], (16, 512))
    bias_push = send(BQ.at[c], BQ.at[c], bq_s.at[0], bq_r.at[0], other)
    bias_push.start()
    for j in range(8):
        wq_push(j).start()
    for q in range(8):
        wo_push(q).start()
    ACC[...] = jnp.zeros_like(ACC)
    for b in range(8):
        line = jnp.broadcast_to(ends[:, b * 128 : (b + 1) * 128].astype(F32), (128, 128))
        E[b] = line.T
    lane = lax.broadcasted_iota(jnp.int32, (8, 512), 1)
    token = lane + lax.div(lane, 64) * 64
    KID[:, 0:512] = token.astype(F32)
    KID[:, 512:1024] = (token + 64).astype(F32)
    KV[:, 256:384] = jnp.ones((1024, 128), BF)
    for n, b in enumerate(order):
        END[n * 64 : (n + 1) * 64, :] = E[b, pl.ds(mo(c * 64, 64), 64), :]

    def project(first, last, j):
        rows = slice(first * 64, last * 64)
        normed = jnp.concatenate(
            [G[j, pl.ds(mo(b * 64, 64), 64), :] for b in order[first:last]], axis=0
        )
        for n in range(2):
            columns = slice(n * 512, (n + 1) * 512)
            ACC[rows, columns] += jnp.dot(normed, WQ[j, :, columns], preferred_element_type=F32)

    def queries(first, last):
        rows = slice(first * 64, last * 64)
        for n in range(2):
            columns = slice(n * 512, (n + 1) * 512)
            Q[rows, columns] = (ACC[rows, columns] + BQ[n, 0:1, :].astype(F32)).astype(BF)

    gathered(0, block(1, 0))
    gather(5, block(1, 0)).start()
    gathered(1, block(3, 0))
    gather(6, block(3, 0)).start()
    gathered(2, block(1, 0))
    gather(3, block(1, 0)).start()
    gathered(2, block(3, 0))
    gather(4, block(3, 0)).start()
    gathered(0, block(1, 1))
    gather(5, block(1, 1)).start()
    gathered(1, block(3, 1))
    gather(6, block(3, 1)).start()
    for n in range(8):
        for kind in range(2):
            if n >= UP_FRONT[kind]:
                gather(kind, own_order[kind][n]).start()
    gathered(5, block(0, 1))
    gathered(6, block(0, 1))
    gather(7, block(0, 1)).start()
    for n in range(UP_FRONT[2], 8):
        gather(2, own_order[2][n]).start()
    gathered(0, own)
    gather(5, own).start()
    gathered(1, own)
    gather(6, own).start()
    for kind in range(2, 8):
        gathered(kind, own)

    for n, w in enumerate((wk, wv)):
        kv_local(w, n).wait()
        part = WKV.at[n, pl.ds(mo((1 - c) * 512, 512), 512), :]
        send(part, part, wkv_s.at[n], wkv_r.at[n], other).wait_recv()
        for m in range(2):
            sums = jnp.dot(
                G[own], WKV[n, :, m * 512 : (m + 1) * 512], preferred_element_type=F32
            ).astype(BF)
            for b in range(4):
                KVT[m * 4 + b, :, n * HEAD : (n + 1) * HEAD] = sums[:, b * HEAD : (b + 1) * HEAD]
    for kind in (7, 3, 4):
        kv_sum(kind).start()

    def pass_along(j, carry):
        @pl.when((j != block(1, 0)) & (j != block(1, 1)) & (j != own))
        def _():
            gathered(0, j)
            gather(5, j).start()

        @pl.when((j != block(3, 0)) & (j != block(3, 1)) & (j != own))
        def _():
            gathered(1, j)
            gather(6, j).start()

        return carry

    lax.fori_loop(0, 8, pass_along, 0)
    gather_side(3).start()
    gather_side(4).start()
    gather_half_side(3).start()
    gather_half_side(4).start()

    def pass_across(j, carry):
        @pl.when((j != block(1, 0)) & (j != block(3, 0)) & (j != own))
        def _():
            gathered(2, j)

        @pl.when((j != block(1, 0)) & (j != block(0, 1)) & (j != block(2, 1)))
        def _():
            gather(3, j).start()

        @pl.when((j != block(3, 0)) & (j != block(0, 1)) & (j != block(2, 1)))
        def _():
            gather(4, j).start()

        @pl.when(j == block(2, 1))
        def _():
            gather_half(3).start()
            gather_half(4).start()

        @pl.when(j != block(0, 1))
        def _():
            @pl.when(j != own)
            def _():
                gathered(5, j)
                gathered(6, j)

            gather(7, j).start()

        @pl.when(j == KV_STEPS[0])
        def _():
            b = block(2, 0)
            KVT[b] = (KVT[b].astype(F32) + kv_came(7)).astype(BF)
            kv_sum(5).start()
            kv_sum(6).start()
            b = block(0, 1)
            KVT[b] = (KVT[b].astype(F32) + kv_came(3) + kv_came(4)).astype(BF)
            kv_sum(2).start()

        @pl.when(j == KV_STEPS[1])
        def _():
            b = block(3, 0)
            KVT[b, 0:256, :] = (KVT[b, 0:256, :].astype(F32) + kv_came(5)).astype(BF)
            kv_sum(0).start()
            b = block(1, 0)
            KVT[b, 256:512, :] = (KVT[b, 256:512, :].astype(F32) + kv_came(6)).astype(BF)
            kv_sum(1).start()

        wq_local(j).wait()
        part = WQ.at[j, :, pl.ds(mo((1 - c) * 512, 512), 512)]
        send(part, part, wq_s.at[j], wq_r.at[j], other).wait_recv()
        project(4, 8, j)
        return carry

    lax.fori_loop(0, 8, pass_across, 0)

    def project_far(j, carry):
        @pl.when(j != own)
        def _():
            gathered(7, j)

        project(2, 4, j)

        @pl.when(j != own)
        def _():
            gathered_side(3, j)
            gathered_side(4, j)

        project(0, 2, j)
        for kind in (0, 1, 2, 5, 6, 7):
            gather(kind, j).wait_send()

        @pl.when(j != block(2, 1))
        def _():
            gather(3, j).wait_send()
            gather(4, j).wait_send()

        @pl.when(j == block(2, 1))
        def _():
            for kind in (3, 4):
                gather_half(kind).wait_send()
                gather_half_side(kind).wait_send()

        @pl.when(j == KV_STEPS[2])
        def _():
            total = KVT[own].astype(F32) + kv_came(0) + kv_came(1) + kv_came(2)
            rows = pl.ds(mo(c * 512, 512), 512)
            KV[rows, 0:HEAD] = total[:, 0:HEAD].astype(BF)
            bias = bv[:, pl.ds(mo(chip * HEAD, HEAD), HEAD)].astype(F32)
            KV[rows, HEAD : 2 * HEAD] = (total[:, HEAD:] + bias).astype(BF)
            part = KV.at[rows, 0 : 2 * HEAD]
            send(part, part, kv_s.at[0], kv_r.at[0], other).start()

        return carry

    lax.fori_loop(0, 8, project_far, 0)

    for to in (yp, ym, xx):
        pl.semaphore_signal(free, inc=1, device_id={"tensor": to}, device_id_type=MESH)
    send(BQ.at[1 - c], BQ.at[1 - c], bq_s.at[0], bq_r.at[0], other).wait_recv()
    queries(0, 2)
    part = KV.at[pl.ds(mo((1 - c) * 512, 512), 512), 0 : 2 * HEAD]
    send(part, part, kv_s.at[0], kv_r.at[0], other).wait_recv()

    def attend(first, last, head, heads):
        rows = slice(first * 64, last * 64)
        columns = [pl.ds(mo((head + n) * HEAD, HEAD), HEAD) for n in range(heads)]
        query = jnp.concatenate([Q[rows, at] for at in columns], axis=0)
        end = jnp.concatenate([END[rows, 0:1]] * heads, axis=0)
        scores = lax.dot_general(
            query, KV[:, 0:HEAD], (((1,), (1,)), ((), ())), preferred_element_type=F32
        )
        scores = jnp.where(KID[0:1, :] < end, scores, -1e30 * HEAD**0.5)
        top = jnp.max(scores, axis=-1, keepdims=True)
        expo = jnp.exp2((scores - top) * (LOG2E / HEAD**0.5)).astype(BF)
        mixed = jnp.dot(expo, KV[:, HEAD : 3 * HEAD], preferred_element_type=F32)
        mixed = (mixed[:, :HEAD] / mixed[:, HEAD:]).astype(BF)
        count = (last - first) * 64
        for n, at in enumerate(columns):
            CTX[rows, at] = mixed[n * count : (n + 1) * count]

    def terms(first, last, k):
        rows = slice(first * 64, last * 64)
        WQ[k, rows, :] = jnp.dot(CTX[rows, :], WO[k], preferred_element_type=F32).astype(BF)

    def attend_two(first):
        def group(n, carry):
            attend(first, first + 2, n * STACK, STACK)
            return carry

        lax.fori_loop(0, 8 // STACK, group, 0)

    def side(k):
        wo_local(k).wait()
        part = WO.at[k, pl.ds(mo((1 - c) * 512, 512), 512), :]
        send(part, part, wo_s.at[k], wo_r.at[k], other).wait_recv()
        terms(0, 2, k)
        reduce(3, k).start()
        reduce(4, k).start()

    attend_two(0)
    pl.semaphore_wait(free, 3)
    for k in range(FIRST):
        side(k)
    queries(2, 8)
    attend_two(2)

    def step(i, carry):
        @pl.when(i < 8)
        def _():
            terms(2, 4, i)
            reduce(7, i).start()

        @pl.when(i < 8 - FIRST)
        def _():
            side(i + FIRST)

        @pl.when(i < 4)
        def _():
            attend(4, 8, 2 * i, 2)

        def at(steps, work):
            @pl.when((i >= steps) & (i < 8 + steps))
            def _():
                work(i - steps)

        at(STEPS[0], opposite)
        at(STEPS[1], across)
        at(STEPS[2], near)
        at(STEPS[3], finish)
        return carry

    def opposite(k):
        WQ[k, 192:256, :] = (term(k, 192) + arrived(7, k)).astype(BF)
        reduce(5, k).start()
        reduce(6, k).start()

    def across(k):
        terms(4, 8, k)
        WQ[k, 256:320, :] = (term(k, 256) + arrived(3, k) + arrived(4, k)).astype(BF)
        reduce(2, k).start()

    def near(k):
        WQ[k, 384:416, :] = (term(k, 384, 32) + arrived(5, k)).astype(BF)
        reduce(0, k).start()
        WQ[k, 352:384, :] = (term(k, 352, 32) + arrived(6, k)).astype(BF)
        reduce(1, k).start()

    def finish(k):
        columns = pl.ds(mo(k * 1024, 1024), 1024)
        total = term(k, 448) + arrived(0, k) + arrived(1, k) + arrived(2, k)
        STG[:, columns] = (HID[:, columns].astype(F32) + total).astype(BF)

        @pl.when(last & (k < RELAYED))
        def _():
            relay_in(k).start()

        @pl.when(jnp.logical_not(last & (k < RELAYED)))
        def _():
            hand(k).start()

        @pl.when(first & (k >= 2) & (k < 2 + RELAYED))
        def _():
            relay_in(k - 2).wait_recv()
            relay_out(k - 2).start()

    lax.fori_loop(0, 8 + STEPS[3], step, 0)

    def sent(k, carry):
        for kind in range(8):
            reduce(kind, k).wait_send()
        hand(k).wait_send()

        @pl.when(first & (k < RELAYED))
        def _():
            relay_out(k).wait_send()

        return carry

    lax.fori_loop(0, 8, sent, 0)
    for n, w in enumerate((wk, wv)):
        kv_push(w, n).wait_send()
    for kind in range(8):
        kv_sum(kind).wait_send()
    for j in range(8):
        wq_push(j).wait_send()
    for q in range(8):
        wo_push(q).wait_send()
    bias_push.wait_send()
    part = KV.at[pl.ds(mo(c * 512, 512), 512), 0 : 2 * HEAD]
    send(part, part, kv_s.at[0], kv_r.at[0], other).wait_send()


    def handed(k, carry):
        hand(k).wait_recv()
        return carry

    lax.fori_loop(0, 8, handed, 0)


def on_device(
    hidden_in, norm_gain, w_query, bias_query, w_key, w_value, bias_value, w_out, visible_end
):
    vmem, anywhere = pl.BlockSpec(memory_space=pltpu.VMEM), pl.BlockSpec(memory_space=pl.ANY)
    dma = pltpu.SemaphoreType.DMA
    return pl.pallas_call(
        layer,
        out_shape=jax.ShapeDtypeStruct(hidden_in.shape, BF),
        in_specs=[anywhere, vmem, anywhere, vmem, anywhere, anywhere, vmem, anywhere, vmem],
        out_specs=anywhere,
        scratch_shapes=[
            pltpu.VMEM((8, 512, 1024), BF),
            pltpu.VMEM((8, 1024, 1024), BF),
            pltpu.VMEM((2, 1024, 1024), BF),
            pltpu.VMEM((8, 1024, 1024), BF),
            pltpu.VMEM((512, 1024), F32),
            pltpu.VMEM((8, 512, 256), BF),
            pltpu.VMEM((7, 512, 256), BF),
            pltpu.VMEM((512, 1024), BF),
            pltpu.VMEM((1024, 384), BF),
            pltpu.VMEM((512, 1024), BF),
            pltpu.VMEM((2, 16, 512), BF),
            pltpu.VMEM((8, 128, 128), F32),
            pltpu.VMEM((512, 128), F32),
            pltpu.VMEM((8, 1024), F32),
            pltpu.VMEM((64, 8192), BF),
            pltpu.VMEM((64, 8192), BF),
            pltpu.VMEM((RELAYED, 64, 1024), BF),
            dma((8, 8)), dma((8, 8)), dma((8, 8)), dma((8, 8)), dma((8,)), dma((8,)), dma((8,)), dma((8,)),
            dma((2,)), dma((2,)),
            dma((1,)), dma((2,)), dma((2,)), dma((2,)), dma((8,)), dma((8,)),
            dma((8,)), dma((8,)), dma((8,)), dma((8,)), dma((8,)), dma((8,)),
            dma((1,)), dma((1,)), dma((1,)), dma((1,)), pltpu.SemaphoreType.REGULAR,
        ],
        compiler_params=pltpu.CompilerParams(
            collective_id=0, has_side_effects=True, vmem_limit_bytes=63 * 2**20
        ),
        cost_estimate=pl.CostEstimate(flops=24 * 10**9, bytes_accessed=40 * 10**6, transcendentals=4 * 2**20),
    )(
        hidden_in, norm_gain, w_query, bias_query, w_key, w_value, bias_value, w_out, visible_end
    )


def solution(mesh):
    placed = (
        P("section", "tensor", None),
        P("section", None),
        P("section", None, "tensor"),
        P("section", "tensor"),
        P("section", "tensor", None),
        P("section", "tensor", None),
        P("section", None),
        P("section", "tensor", None),
        P("section", None),
    )
    return jax.shard_map(
        on_device,
        mesh=mesh,
        in_specs=placed,
        out_specs=P("section", "tensor", None),
        check_vma=False,
    )
```
